512 devices in a mesh: fsdp: 16 (over z, y_lo), ctx: 32 (over y_hi, x, core).
Axes of the slice: x: 4, y: 8 (y_hi: 4, y_lo: 2; y = y_hi * 2 + y_lo), z: 8, core: 2. Of those that a mesh axis runs over, the one named last changes fastest.
Arguments:
- hidden: bfloat16 [16, 4096, 8192], P('fsdp', 'ctx'), may hold values from -6 to 6
- values: bfloat16 [16, 4096, 4096], P('fsdp', 'ctx'), may hold values from -6 to 6
- targets: bfloat16 [16, 4096, 4096], P('fsdp', 'ctx'), may hold values from -6 to 6
- dt_raw: float32 [16, 32, 4096], P('fsdp', None, 'ctx'), as said below
- proj_weight: bfloat16 [8192, 128], P('fsdp'), may hold values from -0.0234375 to 0.0234375
- a_log: float32 [32], replicated
- skip: float32 [32], replicated, may hold values from 0.5 to 1.5
Outputs:
- grad_w: float32 [8192, 128], P('fsdp')
- grad_a_log: float32 [32], replicated
- grad_skip: float32 [32], replicated
- loss: float32 [], replicated
The draws below stay inside these ranges and needn't reach their ends.
Inputs may be any that keep to these rules, and one draw needn't show every extreme that they name: softplus(dt_raw) is the step size of a head at a position.
All inputs are finite; a program needn't handle non-finite values.
Results may differ from the reference program's by a relative error of at most 0.004.
Values may be sent and summed in bfloat16 or wider, within the bound.
A program may use at most 192 MiB of HBM per device.

```python
import math
import jax
import jax.numpy as jnp
from jax import lax

D = 8192
HEADS = 32
HDIM = 128
STATE = 64
TOK_DEV = 128
SEQS = 16
LEN = 4096
INNER = 4096


def draw_dt_raw(key, part):
    first, second = jax.random.split(jax.random.fold_in(key, 11))
    blocks = LEN // TOK_DEV
    device_scale = jnp.exp(jax.random.uniform(first, (SEQS, 1, blocks, 1), jnp.float32, -0.7, 0.7))
    cell_scale = jnp.exp(jax.random.uniform(second, (SEQS, HEADS, blocks, TOK_DEV), jnp.float32, -0.7, 0.7))
    step_size = 1.5 / math.sqrt(LEN) * device_scale * cell_scale
    step_size = step_size.reshape(SEQS, HEADS, LEN)
    return jnp.log(jnp.expm1(step_size))


def draw_a_log(key, part):
    spot = jax.random.uniform(jax.random.fold_in(key, 23), (HEADS,), jnp.float32)
    spot = spot ** 3
    per_step = jnp.exp(spot * math.log(max(LEN / 30.0, 4.0))) / LEN
    rate = per_step * math.sqrt(LEN) / 1.5
    return jnp.log(rate)


def raised(entries, key, source, target, parts, factor):
    def block_of(axis_at):
        return (jnp.arange(entries.shape[axis_at]) // (entries.shape[axis_at] // parts)).reshape((-1,) + (1,) * (entries.ndim - 1 - axis_at))

    first = jax.random.permutation(key, parts)[block_of(target)]
    second = (block_of(target) + parts // 2) % parts
    return jnp.where((block_of(source) == first) | (block_of(source) == second), factor * entries, entries)


def levels(rng, extent, cuts, least, high):
    loudness, own = 1.0, jax.random.fold_in(rng, 6)
    for dim, parts in cuts:
        heights = jnp.exp(jax.random.uniform(jax.random.fold_in(own, dim), (parts,), jnp.float32, least / len(cuts), high / len(cuts)))
        loudness = loudness * jnp.repeat(heights, extent[dim] // parts).reshape([-1 if axis == dim else 1 for axis in range(len(extent))])
    return loudness


def bell_draw(own_key, extent, deviation, reach, shards=(), held_as=jnp.bfloat16):
    level = levels(own_key, extent, shards, -0.22, 0.18) if shards else 1.0
    drawn = jax.random.normal(own_key, extent, jnp.float32) * deviation * level
    return jnp.minimum(jnp.maximum(drawn, -reach), reach).astype(held_as)


def heavy_noise(key, extent, deviation, limit, shards, heavy, kind=jnp.bfloat16):
    drawn = deviation * jax.random.normal(key, extent, jnp.float32)
    if shards:
        drawn = drawn * levels(key, extent, shards, -0.22, 0.18)
    return jnp.clip(raised(drawn, jax.random.fold_in(key, 3), *heavy), -limit, limit).astype(kind)


def setup_inputs(seed: int = 0) -> dict:
    splits = jax.random.split(jax.random.key(seed), 8)
    hidden = heavy_noise(splits[0], (SEQS, LEN, D), 1.0, 6.0, ((0, 16), (1, 32)), (0, 2, 16, 2.0))
    values = bell_draw(splits[1], (SEQS, LEN, INNER), 1.0, 6.0, ((0, 16), (1, 32)))
    targets = bell_draw(splits[2], (SEQS, LEN, INNER), 1.0, 6.0, ((0, 16), (1, 32)))
    dt_raw = draw_dt_raw(jax.random.fold_in(splits[7], 71), 0)
    proj_weight = bell_draw(splits[4], (D, 2 * STATE), (8 * D) ** -0.5, 0.0234375, ((0, 16),))
    a_log = draw_a_log(jax.random.fold_in(splits[7], 71), 0)
    skip = jnp.clip(jax.random.uniform(splits[6], (HEADS,), jnp.float32, 0.5, 1.5), 0.5, 1.5)
    return dict(hidden=hidden, values=values, targets=targets, dt_raw=dt_raw, proj_weight=proj_weight, a_log=a_log, skip=skip)


highest = lax.Precision.HIGHEST

def product(form, left, right):
    left, right = lax.optimization_barrier((left, right))
    return jnp.einsum(form, left.astype(jnp.float32), right.astype(jnp.float32), precision=highest)

def block_local(proj, step_size, decay_rate, vals, lower_mask):
    row_count = proj.shape[0]
    head_count = step_size.shape[0]
    state_width = proj.shape[1] // 2
    input_map = proj[:, :state_width]
    output_map = proj[:, state_width:]
    decay_sum = jnp.cumsum(step_size * decay_rate[:, None], axis=1)
    final = decay_sum[:, -1:]
    scores = jnp.dot(output_map, input_map.T, preferred_element_type=jnp.float32)
    within = jnp.where(lower_mask[None] > 0, jnp.exp(jnp.minimum(decay_sum[:, :, None] - decay_sum[:, None, :], 0.0)), 0.0)
    mixing = within * scores[None] * step_size[:, None, :]
    inputs = vals.reshape(row_count, head_count, vals.shape[1] // head_count)
    inner_out = product('hts,shp->thp', mixing.astype(jnp.bfloat16), inputs)
    to_end = jnp.exp(final - decay_sum)
    weight_end = to_end * step_size
    coef = (weight_end[:, None, :] * input_map.T.astype(jnp.float32)[None]).astype(jnp.bfloat16)
    local_state = product('hns,shp->hnp', coef, inputs)
    growth = jnp.exp(decay_sum)
    carry = jnp.exp(final[:, 0])
    return (input_map, output_map, step_size, decay_sum, within, mixing, inputs, to_end, weight_end, growth, local_state, carry, inner_out)

def block_output(pack, state_in, wanted, skip_gain):
    input_map, output_map, step_size, decay_sum, within, mixing, inputs, to_end, weight_end, growth, local_state, carry, inner_out = pack
    state_bf = state_in.astype(jnp.bfloat16)
    from_state = product('hnp,tn->thp', state_bf, output_map)
    outputs = inner_out + growth.T[:, :, None] * from_state + skip_gain[None, :, None] * inputs.astype(jnp.float32)
    misfit = outputs - wanted.reshape(inputs.shape).astype(jnp.float32)
    return (misfit, from_state, state_bf)

def block_return(pack, from_state, state_bf, misfit, loss_scale):
    input_map, output_map, step_size, decay_sum, within, mixing, inputs, to_end, weight_end, growth, local_state, carry, inner_out = pack
    grad_out = misfit * loss_scale
    skip_part = lax.optimization_barrier(jnp.sum(grad_out * inputs.astype(jnp.float32), axis=(0, 2)))
    grad_bf = grad_out.astype(jnp.bfloat16)
    mix_grad = product('thp,shp->hts', grad_bf, inputs)
    score_grad = lax.optimization_barrier(jnp.sum(within * mix_grad * step_size[:, None, :], axis=0))
    weighted = mix_grad * mixing
    sum_grad = lax.optimization_barrier(jnp.sum(weighted, axis=2)) - lax.optimization_barrier(jnp.sum(weighted, axis=1)) + growth * lax.optimization_barrier(jnp.sum(grad_out * from_state, axis=2)).T
    grown_bf = (growth.T[:, :, None] * grad_out).astype(jnp.bfloat16)
    entry_grad = product('thp,tn->hnp', grown_bf, output_map)
    score_bf = score_grad.astype(jnp.bfloat16)
    out_grad = product('thp,hnp->tn', grown_bf, state_bf) + product('ts,sn->tn', score_bf, input_map)
    in_grad = product('ts,tn->sn', score_bf, output_map)
    return (entry_grad, (out_grad, in_grad, sum_grad, skip_part))

def block_finish(pack, partial_value, exit_grad, state_in, decay_rate):
    input_map, output_map, step_size, decay_sum, within, mixing, inputs, to_end, weight_end, growth, local_state, carry, inner_out = pack
    out_grad, in_grad, sum_grad, skip_part = partial_value
    exit_bf = exit_grad.astype(jnp.bfloat16)
    coef_grad = product('hnp,shp->hns', exit_bf, inputs)
    in_grad = in_grad + jnp.einsum('hns,hs->sn', coef_grad, weight_end, precision=highest)
    pulled = jnp.einsum('hns,sn->hs', coef_grad, input_map.astype(jnp.float32), precision=highest)
    end_weight = pulled * weight_end
    final_grad = lax.optimization_barrier(jnp.sum(end_weight, axis=1)) + carry * lax.optimization_barrier(jnp.sum(exit_grad * state_in, axis=(1, 2)))
    row_count = step_size.shape[1]
    last_mark = (jnp.arange(row_count) == row_count - 1).astype(jnp.float32)
    sum_grad = sum_grad - end_weight + final_grad[:, None] * last_mark[None, :]
    step_grad = jnp.cumsum(sum_grad[:, ::-1], axis=1)[:, ::-1]
    alog_part = decay_rate * lax.optimization_barrier(jnp.sum(step_grad * step_size, axis=1))
    proj_grad = jnp.concatenate([in_grad, out_grad], axis=1).astype(jnp.bfloat16)
    return (proj_grad, alog_part, skip_part)

def reference(hidden, values, targets, dt_raw, proj_weight, a_log, skip):
    flat_rows = hidden.reshape(SEQS * LEN, D)
    projection = jnp.dot(flat_rows, proj_weight, preferred_element_type=jnp.float32).astype(jnp.bfloat16)
    projection = projection.reshape(SEQS, LEN, 2 * STATE)
    decay_rate = -jnp.exp(a_log)
    loss_scale = 1.0 / (INNER * math.sqrt(SEQS * LEN))
    blocks = LEN // TOK_DEV
    position = jnp.arange(TOK_DEV)
    lower_mask = (position[:, None] >= position[None, :]).astype(jnp.float32)

    def one_sequence(totals, seq_items):
        proj_s, raw_s, vals_s, goal_s = seq_items
        step_all = jax.nn.softplus(raw_s)
        proj_b = proj_s.reshape(blocks, TOK_DEV, 2 * STATE)
        step_b = step_all.reshape(HEADS, blocks, TOK_DEV).transpose(1, 0, 2)
        vals_b = vals_s.reshape(blocks, TOK_DEV, INNER)
        goal_b = goal_s.reshape(blocks, TOK_DEV, INNER)

        def advance(state_in, block_items):
            proj_k, step_k, vals_k, goal_k = block_items
            local_pack = block_local(proj_k, step_k, decay_rate, vals_k, lower_mask)
            misfit, from_state, state_bf = block_output(local_pack, state_in, goal_k, skip)
            entry_grad, partial_value = block_return(local_pack, from_state, state_bf, misfit, loss_scale)
            new_state = local_pack[11][:, None, None] * state_in + local_pack[10]
            return (new_state, (state_in, local_pack[11], entry_grad, jnp.sum(misfit * misfit)))
        zero_state = jnp.zeros((HEADS, STATE, HDIM), jnp.float32)
        ignored, (state_ins, carries, entry_grads, squares) = lax.scan(advance, zero_state, (proj_b, step_b, vals_b, goal_b))

        def retreat(exit_now, block_items):
            carry_k, entry_k = block_items
            return (entry_k + carry_k[:, None, None] * exit_now, exit_now)
        unused, exit_grads = lax.scan(retreat, zero_state, (carries, entry_grads), reverse=True)

        def finish(block_items):
            proj_k, step_k, vals_k, goal_k, state_k, exit_k = block_items
            local_pack = block_local(proj_k, step_k, decay_rate, vals_k, lower_mask)
            misfit, from_state, state_bf = block_output(local_pack, state_k, goal_k, skip)
            entry_grad, partial_value = block_return(local_pack, from_state, state_bf, misfit, loss_scale)
            return block_finish(local_pack, partial_value, exit_k, state_k, decay_rate)
        proj_grads, alog_parts, skip_parts = lax.map(finish, (proj_b, step_b, vals_b, goal_b, state_ins, exit_grads))
        loss_value = 0.5 * loss_scale * jnp.sum(squares)
        updated = (totals[0] + loss_value, totals[1] + lax.optimization_barrier(jnp.sum(alog_parts, axis=0)), totals[2] + lax.optimization_barrier(jnp.sum(skip_parts, axis=0)))
        return (updated, proj_grads.reshape(LEN, 2 * STATE))
    begin = (jnp.zeros((), jnp.float32), jnp.zeros((HEADS,), jnp.float32), jnp.zeros((HEADS,), jnp.float32))
    totals, all_grads = lax.scan(one_sequence, begin, (projection, dt_raw, values, targets))
    grad_w = lax.dot_general(flat_rows, all_grads.reshape(SEQS * LEN, 2 * STATE), (((0,), (0,)), ((), ())), preferred_element_type=jnp.float32)
    return (grad_w, totals[1], totals[2], totals[0])
```

```python
import functools
import math

import jax
import jax.numpy as jnp
from jax import lax
from jax.experimental import pallas as pl
from jax.experimental.pallas import tpu as pltpu
from jax.sharding import PartitionSpec as P

HIGHEST = lax.Precision.HIGHEST
MESH = pl.DeviceIdType.MESH
F32 = jnp.float32
BF16 = jnp.bfloat16
T = 128
N = 64
ROW_CHIPS = 4


def dot(left, right):
    return jnp.dot(left, right, preferred_element_type=F32)


def dot_last(left, right):
    return lax.dot_general(left, right, (((1,), (1,)), ((), ())), preferred_element_type=F32)


def body(
    shards, blocks, scale,
    hid, val, tgt, dt, w, par, ow, osc,
    wbuf, hq, ws, dcb, bs, step_s, decay_s, fin_s, we_s, alog_s, skip_s, loss_s,
    carry_out, carry_in, l_out, l_in, s_out, s_in, e_out, e_in, x_out, x_in,
    sg, acc_c, acc_b, pg_out, pg_in, r_out, r_in, c_out, c_in, y_out, y_in, z_out, z_in,
    w_send, w_recv, v_send, v_recv, h_send, h_own, h_fwd, h_recv, k_send, k_recv,
    l_send, l_recv, s_send, s_recv, e_send, e_recv, x_send, x_recv,
    p_send, p_recv, r_send, r_recv, c_send, c_recv, y_send, y_recv, z_send, z_recv,
):
    heads = dt.shape[0]
    wide = w.shape[0]
    half = wide // 2
    chips = ROW_CHIPS
    octet = 2 * chips
    rows = blocks // octet
    f = lax.axis_index("fsdp")
    k = lax.axis_index("ctx")
    c = lax.rem(k, 2)
    o = lax.rem(k, octet)
    yh = lax.div(k, octet)
    x = lax.div(o, 2)
    first = yh * octet
    sib = k + 1 - 2 * c

    def ring(start, hop, count):
        return lax.rem(start + hop, count)

    def remote(src, dst, ss, rs, to_f, to_k):
        return pltpu.make_async_remote_copy(
            src_ref=src, dst_ref=dst, send_sem=ss, recv_sem=rs,
            device_id=(to_f, to_k), device_id_type=MESH,
        )

    def arrived(dst, rs):
        remote(dst, dst, rs, rs, f, sib).wait_recv()

    def left(src, ss):
        remote(src, src, ss, ss, f, sib).wait_send()

    def loop(count, fn, start=0):
        def step(i, carry):
            fn(i)
            return carry

        lax.fori_loop(start, count, step, 0)

    def lanes(i):
        return pl.ds(pl.multiple_of(i * T, T), T)

    barrier = pltpu.get_barrier_semaphore()

    def greet_f(j):
        pl.semaphore_signal(barrier, inc=1, device_id=(ring(f, j, shards), k), device_id_type=MESH)

    def greet_k(j):
        pl.semaphore_signal(barrier, inc=1, device_id=(f, ring(k, j, blocks)), device_id_type=MESH)

    loop(shards, greet_f, 1)
    loop(blocks, greet_k, 1)
    pl.semaphore_wait(barrier, shards + blocks - 2)

    def w_rows(g, core):
        return pl.ds(pl.multiple_of(g * wide + core * half, half), half)

    def w_go(j):
        remote(
            w.at[pl.ds(pl.multiple_of(c * half, half), half)], wbuf.at[w_rows(f, c)],
            w_send, w_recv.at[f], ring(f, j, shards), k,
        ).start()

    loop(shards, w_go, 1)

    step = jnp.maximum(dt[...], 0.0) + jnp.log1p(jnp.exp(-jnp.abs(dt[...])))
    row_id = lax.broadcasted_iota(jnp.int32, (T, T), 0)
    col_id = lax.broadcasted_iota(jnp.int32, (T, T), 1)
    upper = jnp.where(row_id <= col_id, 1.0, 0.0).astype(F32)
    decay = jnp.dot(-step * jnp.exp(par[0]), upper, precision=HIGHEST, preferred_element_type=F32)
    fin = jnp.broadcast_to(decay[:, T - 1 :], (heads, T))
    step_s[...] = step
    decay_s[...] = decay
    fin_s[...] = fin
    we_s[...] = jnp.exp(fin - decay) * step

    def carry_go(h):
        carry_out[h] = jnp.broadcast_to(jnp.exp(fin_s[pl.ds(h, 1), :]), (8, T))

        @pl.when(h != k)
        def _():
            remote(carry_out.at[h], carry_in.at[k], k_send, k_recv.at[k], f, h).start()

        @pl.when(h == k)
        def _():
            carry_in[h] = carry_out[h]

    loop(heads, carry_go)

    own_rows = pl.ds(pl.multiple_of(o * T, T), T)

    def h_go(i):
        for hop in range(1, chips):
            there = ring(x, hop, chips)
            remote(
                hid.at[:, pl.ds(pl.multiple_of(i * wide + there * T, T), T)], hq.at[own_rows, lanes(i)],
                h_send, h_recv.at[o], f, first + there * 2 + c,
            ).start()
        hq[own_rows, lanes(i)] = hid[:, pl.ds(pl.multiple_of(i * wide + x * T, T), T)]

    loop(shards, h_go)
    remote(hq.at[own_rows], hq.at[own_rows], h_own, h_recv.at[o], f, sib).start()

    lower = row_id >= col_id

    def head_start(h):
        drow = decay_s[pl.ds(h, 1), :]
        col = jnp.transpose(jnp.broadcast_to(drow, (T, T)))
        dcb[h] = col
        within = jnp.where(lower, jnp.exp(jnp.minimum(col - drow, 0.0)), 0.0)
        ws[h] = within * step_s[pl.ds(h, 1), :]
        gain = par[1, pl.ds(h, 1), :]
        bs[h] = gain * val[:, lanes(h)].astype(F32) - tgt[:, lanes(h)].astype(F32)

    loop(heads, head_start)

    def w_pass(j):
        g = ring(f, j, shards)
        slot = wbuf.at[w_rows(g, c)]
        arrived(slot, w_recv.at[g])
        remote(slot, slot, v_send, v_recv.at[g], f, sib).start()

    loop(shards, w_pass, 1)

    def hid_cols(g):
        return hid[:, pl.ds(pl.multiple_of(g * wide, wide), wide)]

    def w_use(j, total):
        g = ring(f, j, shards)
        arrived(wbuf.at[w_rows(g, 1 - c)], v_recv.at[g])
        return total + dot(hid_cols(g), wbuf[pl.ds(pl.multiple_of(g * wide, wide), wide), :])

    proj = lax.fori_loop(1, shards, w_use, dot(hid_cols(f), w[...]))
    proj = proj.astype(BF16).astype(F32)
    proj_t = jnp.transpose(proj)
    map_bt = proj_t[:N]
    map_b_t = proj_t[:N].astype(BF16)
    map_c_t = proj_t[N:].astype(BF16)
    map_c = proj[:, N:].astype(BF16)
    scores = dot(map_c, map_b_t)

    def head_local(h):
        v = val[:, lanes(h)]
        mixing = (ws[h] * scores).astype(BF16)
        coef = (map_bt * we_s[pl.ds(h, 1), :]).astype(BF16)
        both = dot(jnp.concatenate([mixing, coef], axis=0), v)
        bs[h] = bs[h] + both[:T]
        l_out[h] = both[T:].astype(BF16)

        @pl.when(h != k)
        def _():
            remote(l_out.at[h], l_in.at[k], l_send, l_recv.at[k], f, h).start()

        @pl.when(h == k)
        def _():
            l_in[h] = l_out[h]

    loop(heads, head_local)

    for hop in range(1, chips):
        j = ring(x, hop, chips) * 2 + c
        slab = hq.at[pl.ds(pl.multiple_of(j * T, T), T)]
        arrived(slab, h_recv.at[j])
        remote(slab, slab, h_fwd, h_recv.at[j], f, sib).start()

    def carry_wait(j):
        g = ring(k, j, blocks)
        arrived(carry_in.at[g], k_recv.at[g])

    loop(blocks, carry_wait, 1)

    def chain(came, out, back, in_sem, send_sem, back_sem, backward):
        def link(i, state):
            b = blocks - 1 - i if backward else i
            out[b] = state.astype(BF16)

            @pl.when(b != k)
            def _():
                remote(out.at[b], back.at[k], send_sem, back_sem.at[k], f, b).start()
                arrived(came.at[b], in_sem.at[b])

            @pl.when(b == k)
            def _():
                back[b] = out[b]

            return carry_in[b, 0:1, :] * state + came[b].astype(F32)

        lax.fori_loop(0, blocks, link, jnp.zeros((N, T), F32))

    chain(l_in, s_out, s_in, l_recv, s_send, s_recv, False)

    sg[...] = jnp.zeros_like(sg)
    acc_c[...] = jnp.zeros_like(acc_c)
    acc_b[...] = jnp.zeros_like(acc_b)

    def head_error(h):
        @pl.when(h != k)
        def _():
            arrived(s_in.at[h], s_recv.at[h])

        v = val[:, lanes(h)]
        state = s_in[h]
        col = dcb[h]
        growth = jnp.exp(col)
        grown_state = growth * dot(map_c, state)
        err = bs[h] + grown_state
        grad = err * scale
        loss_s[pl.ds(h, 1), :] = jnp.sum(err * err, axis=0, keepdims=True)
        skip_s[pl.ds(h, 1), :] = jnp.sum(grad * v.astype(F32), axis=0, keepdims=True)
        mix_grad = ws[h] * dot_last(grad.astype(BF16), v)
        sg[...] += mix_grad
        turn = mix_grad * scores * (col - decay_s[pl.ds(h, 1), :]) + grad * grown_state * col
        alog_s[pl.ds(h, 1), :] = jnp.sum(turn, axis=0, keepdims=True)
        grown = (growth * grad).astype(BF16)
        e_out[h] = dot(map_c_t, grown).astype(BF16)
        acc_c[...] += dot_last(state, grown)

        @pl.when(h != k)
        def _():
            remote(e_out.at[h], e_in.at[k], e_send, e_recv.at[k], f, h).start()

        @pl.when(h == k)
        def _():
            e_in[h] = e_out[h]

    loop(heads, head_error)
    chain(e_in, x_out, x_in, e_recv, x_send, x_recv, True)

    def head_exit(h):
        @pl.when(h != k)
        def _():
            arrived(x_in.at[h], x_recv.at[h])

        leaving = x_in[h]
        last = fin_s[pl.ds(h, 1), :]
        weighed = dot_last(leaving, val[:, lanes(h)]) * we_s[pl.ds(h, 1), :]
        acc_b[...] += weighed
        end = jnp.sum(weighed * map_bt, axis=0, keepdims=True)
        kept = jnp.sum(leaving.astype(F32) * s_in[h].astype(F32), axis=0, keepdims=True)
        alog_s[pl.ds(h, 1), :] += end * (last - decay_s[pl.ds(h, 1), :]) + last * jnp.exp(last) * kept

    loop(heads, head_exit)

    score_bf = sg[...].astype(BF16)
    pg_out[0] = (dot(map_c_t, score_bf) + acc_b[...]).astype(BF16)
    pg_out[1] = (dot_last(map_b_t, score_bf) + acc_c[...]).astype(BF16)
    own_cols = lanes(o)

    def pg_go(j):
        there = ring(o, j, octet)
        remote(
            pg_out.at[lax.rem(there, 2)], pg_in.at[:, own_cols], p_send, p_recv.at[o], f, first + there
        ).start()

    loop(octet, pg_go, 1)
    pg_in[:, own_cols] = pg_out[c]

    lane = lax.broadcasted_iota(jnp.int32, (heads, T), 1)
    alog = jnp.sum(alog_s[...], axis=1, keepdims=True)
    skip = jnp.sum(skip_s[...], axis=1, keepdims=True)
    loss = jnp.sum(loss_s[...], axis=1, keepdims=True) * (0.5 * scale)
    c_out[...] = jnp.where(lane == 0, alog, jnp.where(lane == 1, skip, jnp.where(lane == 2, loss, 0.0)))

    def c_go(j):
        remote(c_out, c_in.at[f], c_send, c_recv.at[f], ring(f, j, shards), k).start()

    loop(shards, c_go, 1)
    c_in[f] = c_out[...]

    def h_wait(j):
        src = j * 2 + 1 - c
        arrived(hq.at[pl.ds(pl.multiple_of(src * T, T), T)], h_recv.at[src])

    loop(chips, h_wait)

    def pg_wait(j):
        src = ring(o, j, octet)
        arrived(pg_in.at[:, lanes(src)], p_recv.at[src])

    loop(octet, pg_wait, 1)

    def r_go(j):
        g = ring(f, j, shards)
        r_out[g] = dot(pg_in[...], hq[:, lanes(g)]).astype(BF16)

        @pl.when(g != f)
        def _():
            remote(r_out.at[g], r_in.at[f], r_send, r_recv.at[f], g, k).start()

        @pl.when(g == f)
        def _():
            r_in[g] = r_out[g]

    loop(shards + 1, r_go, 1)

    def r_wait(j):
        g = ring(f, j, shards)
        arrived(r_in.at[g], r_recv.at[g])
        arrived(c_in.at[g], c_recv.at[g])

    loop(shards, r_wait, 1)
    y_out[0:N, :] = lax.fori_loop(0, shards, lambda i, s: s + r_in[i].astype(F32), jnp.zeros((N, T), F32))
    y_out[N:, :] = lax.fori_loop(0, shards, lambda i, s: s + c_in[i], jnp.zeros((heads, T), F32))

    for hop in range(1, rows):
        remote(y_out, y_in.at[yh], y_send.at[hop], y_recv.at[yh], f, ring(yh, hop, rows) * octet + o).start()
    y_in[yh] = y_out[...]
    for hop in range(1, rows):
        src = ring(yh, hop, rows)
        arrived(y_in.at[src], y_recv.at[src])
    total = y_in[0]
    for i in range(1, rows):
        total = total + y_in[i]
    z_out[...] = total

    def z_go(j):
        remote(z_out, z_in.at[o], z_send, z_recv.at[o], f, first + ring(o, j, octet)).start()

    loop(octet, z_go, 1)
    z_in[o] = z_out[...]

    def z_wait(j):
        src = ring(o, j, octet)
        arrived(z_in.at[src], z_recv.at[src])

    loop(octet, z_wait, 1)
    for i in range(chips):
        ow[i * T : (i + 1) * T, :] = jnp.transpose(
            jnp.concatenate([z_in[2 * i, 0:N, :], z_in[2 * i + 1, 0:N, :]], axis=0)
        )
    sums = z_in[0, N:, :]
    for i in range(1, octet):
        sums = sums + z_in[i, N:, :]
    osc[...] = sums

    others = pl.ds(0, blocks - 1)
    peers = pl.ds(0, shards - 1)
    left(wbuf.at[pl.ds(0, (shards - 1) * half)], w_send)
    left(wbuf.at[pl.ds(0, (shards - 1) * half)], v_send)
    left(hq.at[pl.ds(0, (chips - 1) * T)], h_send)
    left(hq.at[pl.ds(0, T)], h_own)
    left(hq.at[pl.ds(0, (chips - 1) * T)], h_fwd)
    left(carry_out.at[others], k_send)
    left(l_out.at[others], l_send)
    left(s_out.at[others], s_send)
    left(e_out.at[others], e_send)
    left(x_out.at[others], x_send)
    left(pg_in.at[:, pl.ds(0, (octet - 1) * T)], p_send)
    left(r_out.at[peers], r_send)
    left(c_in.at[peers], c_send)
    for hop in range(1, rows):
        left(y_out, y_send.at[hop])
    left(z_in.at[pl.ds(0, octet - 1)], z_send)


def local(hidden, values, targets, dt_raw, proj_weight, a_log, skip):
    shards = lax.axis_size("fsdp")
    blocks = lax.axis_size("ctx")
    heads = a_log.shape[0]
    wide, both = proj_weight.shape
    octet = 2 * ROW_CHIPS
    rows = blocks // octet
    scale = 1.0 / (values.shape[2] * math.sqrt(shards * hidden.shape[1] * blocks))
    par = jnp.broadcast_to(jnp.stack([a_log, skip])[:, :, None], (2, heads, T))
    vmem = pltpu.VMEM
    per_head = lambda kind: vmem((heads, N, T), kind)
    small = vmem((heads, T), F32)
    one = pltpu.SemaphoreType.DMA
    many = lambda n: pltpu.SemaphoreType.DMA((n,))
    scratch = [
        vmem((shards * wide, both), BF16),
        vmem((octet * T, shards * T), BF16),
        vmem((heads, T, T), F32), vmem((heads, T, T), F32), vmem((heads, T, T), F32),
        small, small, small, small, small, small, small,
        vmem((heads, 8, T), F32), vmem((blocks, 8, T), F32),
        *[per_head(BF16)] * 8,
        vmem((T, T), F32), vmem((N, T), F32), vmem((N, T), F32),
        vmem((2, N, T), BF16), vmem((N, octet * T), BF16),
        vmem((shards, N, T), BF16), vmem((shards, N, T), BF16),
        small, vmem((shards, heads, T), F32),
        vmem((N + heads, T), F32), vmem((rows, N + heads, T), F32),
        vmem((N + heads, T), F32), vmem((octet, N + heads, T), F32),
        one, many(shards), one, many(shards), one, one, one, many(octet), one, many(blocks),
        *[one, many(blocks)] * 4,
        one, many(octet), one, many(shards), one, many(shards), many(rows), many(rows), one, many(octet),
    ]
    spec = pl.BlockSpec(memory_space=vmem)
    grad_w, sums = pl.pallas_call(
        functools.partial(body, shards, blocks, scale),
        out_shape=(
            jax.ShapeDtypeStruct((wide, both), F32),
            jax.ShapeDtypeStruct((heads, T), F32),
        ),
        in_specs=[spec] * 6,
        out_specs=(spec, spec),
        scratch_shapes=scratch,
        compiler_params=pltpu.CompilerParams(
            collective_id=0, has_side_effects=True, vmem_limit_bytes=48 * 2**20
        ),
    )(hidden[0], values[0], targets[0], dt_raw[0], proj_weight, par)
    return (grad_w, sums[:, 0], sums[:, 1], jnp.sum(sums[:, 2]))


def solution(mesh):
    in_specs = (
        P("fsdp", "ctx", None),
        P("fsdp", "ctx", None),
        P("fsdp", "ctx", None),
        P("fsdp", None, "ctx"),
        P("fsdp", None),
        P(),
        P(),
    )
    out_specs = (P("fsdp", None), P(), P(), P())
    return jax.shard_map(local, mesh=mesh, in_specs=in_specs, out_specs=out_specs, check_vma=False)
```

```python
import functools
import math

import jax
import jax.numpy as jnp
from jax import lax
from jax.experimental import pallas as pl
from jax.experimental.pallas import tpu as pltpu
from jax.sharding import PartitionSpec as P

HIGHEST = lax.Precision.HIGHEST
MESH = pl.DeviceIdType.MESH
F32 = jnp.float32
BF16 = jnp.bfloat16
T = 128
N = 64
ROW_CHIPS = 4


def dot(left, right):
    return jnp.dot(left, right, preferred_element_type=F32)


def dot_last(left, right):
    return lax.dot_general(left, right, (((1,), (1,)), ((), ())), preferred_element_type=F32)


def body(
    shards, blocks, scale,
    hid_h, val_h, tgt_h, dt_h, w_h, a_ref, skip_ref, ow, osc,
    hid, val, tgt, dt, w, in_sem, wbuf, hq, ws, dcb, bs, rate_s, step_s, decay_s, fin_s, we_s, alog_s, skip_s, loss_s,
    carry_out, carry_in, l_out, l_in, s_out, s_in, e_out, e_in, x_out, x_in,
    sg, acc_c, acc_b, pg_out, pg_in, r_out, r_in, c_out, c_in, y_out, y_in, z_out, z_in,
    w_send, w_recv, v_send, v_recv, u_send, h_send, h_far, h_own, h_fwd, h_recv, k_send, k_recv,
    l_send, l_recv, s_send, s_recv, e_send, e_recv, x_send, x_recv,
    p_send, p_recv, r_send, r_recv, c_send, c_recv, y_send, y_recv, z_send, z_recv,
):
    heads = dt.shape[0]
    wide = w.shape[0]
    part = wide // (2 * ROW_CHIPS)
    chips = ROW_CHIPS
    octet = 2 * chips
    rows = blocks // octet
    f = lax.axis_index("fsdp")
    k = lax.axis_index("ctx")
    c = lax.rem(k, 2)
    o = lax.rem(k, octet)
    yh = lax.div(k, octet)
    x = lax.div(o, 2)
    first = yh * octet
    sib = k + 1 - 2 * c

    def ring(start, hop, count):
        return lax.rem(start + hop, count)

    def remote(src, dst, ss, rs, to_f, to_k):
        return pltpu.make_async_remote_copy(
            src_ref=src, dst_ref=dst, send_sem=ss, recv_sem=rs,
            device_id=(to_f, to_k), device_id_type=MESH,
        )

    def arrived(dst, rs):
        remote(dst, dst, rs, rs, f, sib).wait_recv()

    def left(src, ss):
        remote(src, src, ss, ss, f, sib).wait_send()

    def loop(count, fn, start=0):
        def step(i, carry):
            fn(i)
            return carry

        lax.fori_loop(start, count, step, 0)

    def lanes(i):
        return pl.ds(pl.multiple_of(i * T, T), T)

    barrier = pltpu.get_barrier_semaphore()

    def greet_f(j):
        pl.semaphore_signal(barrier, inc=1, device_id=(ring(f, j, shards), k), device_id_type=MESH)

    def greet_k(j):
        pl.semaphore_signal(barrier, inc=1, device_id=(f, ring(k, j, blocks)), device_id_type=MESH)

    loop(shards, greet_f, 1)
    loop(blocks, greet_k, 1)
    loads = [
        pltpu.make_async_copy(src, dst, in_sem.at[i])
        for i, (src, dst) in enumerate(((w_h, w), (dt_h, dt), (val_h, val), (tgt_h, tgt), (hid_h, hid)))
    ]
    for load in loads:
        load.start()
    loads[0].wait()
    pl.semaphore_wait(barrier, shards + blocks - 2)

    own_part = pl.ds(pl.multiple_of(o * part, part), part)

    def w_go(j):
        remote(w.at[own_part], wbuf.at[f, own_part], w_send, w_recv.at[f], ring(f, j, shards), k).start()

    loop(shards, w_go, 1)
    wbuf[f, own_part, :] = w[own_part, :]

    loads[1].wait()

    def spread(h):
        rate_s[pl.ds(h, 1), :] = jnp.full((1, T), a_ref[h], F32)

    loop(heads, spread)
    step = jnp.maximum(dt[...], 0.0) + jnp.log1p(jnp.exp(-jnp.abs(dt[...])))
    row_id = lax.broadcasted_iota(jnp.int32, (T, T), 0)
    col_id = lax.broadcasted_iota(jnp.int32, (T, T), 1)
    upper = jnp.where(row_id <= col_id, 1.0, 0.0).astype(F32)
    decay = jnp.dot(-step * jnp.exp(rate_s[...]), upper, precision=HIGHEST, preferred_element_type=F32)
    fin = jnp.broadcast_to(decay[:, T - 1 :], (heads, T))
    step_s[...] = step
    decay_s[...] = decay
    fin_s[...] = fin
    we_s[...] = jnp.exp(fin - decay) * step

    def carry_go(h):
        carry_out[h] = jnp.broadcast_to(jnp.exp(fin_s[pl.ds(h, 1), :]), (8, T))

        @pl.when(h != k)
        def _():
            remote(carry_out.at[h], carry_in.at[k], k_send, k_recv.at[k], f, h).start()

        @pl.when(h == k)
        def _():
            carry_in[h] = carry_out[h]

    loop(heads, carry_go)

    def w_pass(j):
        g = ring(f, shards - j, shards)
        slot = wbuf.at[g, own_part]

        @pl.when(j > 0)
        def _():
            arrived(slot, w_recv.at[g])

        for hop in range(1, chips):
            there = first + ring(x, hop, chips) * 2 + c
            remote(slot, slot, v_send, v_recv.at[o], f, there).start()

    loop(shards, w_pass)
    own_slab = wbuf.at[:, own_part]
    remote(own_slab, own_slab, u_send, v_recv.at[o], f, sib).start()

    own_rows = pl.ds(pl.multiple_of(o * T, T), T)

    def hid_to(i, hop, sem):
        there = ring(x, hop, chips)
        remote(
            hid.at[:, pl.ds(pl.multiple_of(i * wide + there * T, T), T)], hq.at[own_rows, lanes(i)],
            sem, h_recv.at[o], f, first + there * 2 + c,
        ).start()

    loads[4].wait()

    def h_near(i):
        hid_to(i, 1, h_send)
        if chips > 2:
            hid_to(i, chips - 1, h_send)
        hq[own_rows, lanes(i)] = hid[:, pl.ds(pl.multiple_of(i * wide + x * T, T), T)]

    def h_away(i):
        for hop in range(2, chips - 1):
            hid_to(i, hop, h_far)

    loop(shards, h_near)
    remote(hq.at[own_rows], hq.at[own_rows], h_own, h_recv.at[o], f, sib).start()

    loads[2].wait()
    loads[3].wait()
    lower = row_id >= col_id

    def head_start(h):
        drow = decay_s[pl.ds(h, 1), :]
        col = jnp.transpose(jnp.broadcast_to(drow, (T, T)))
        dcb[h] = col
        within = jnp.where(lower, jnp.exp(jnp.minimum(col - drow, 0.0)), 0.0)
        ws[h] = within * step_s[pl.ds(h, 1), :]
        bs[h] = skip_ref[h] * val[:, lanes(h)].astype(F32) - tgt[:, lanes(h)].astype(F32)

    loop(heads, head_start)

    def slab(src):
        return wbuf.at[:, pl.ds(pl.multiple_of(src * part, part), part)]

    for hop in range(1, chips):
        src = ring(x, hop, chips) * 2 + c
        arrived(slab(src), v_recv.at[src])
        remote(slab(src), slab(src), u_send, v_recv.at[src], f, sib).start()

    def w_rest(j):
        src = j * 2 + 1 - c
        arrived(slab(src), v_recv.at[src])

    loop(chips, w_rest)
    proj = dot(hid[...], wbuf[...].reshape(shards * wide, 2 * N))
    proj = proj.astype(BF16).astype(F32)
    proj_t = jnp.transpose(proj)
    map_bt = proj_t[:N]
    map_b_t = proj_t[:N].astype(BF16)
    map_c_t = proj_t[N:].astype(BF16)
    map_c = proj[:, N:].astype(BF16)
    scores = dot(map_c, map_b_t)

    def head_local(j):
        h = ring(k, j, heads)
        v = val[:, lanes(h)]
        mixing = (ws[h] * scores).astype(BF16)
        coef = (map_bt * we_s[pl.ds(h, 1), :]).astype(BF16)
        both = dot(jnp.concatenate([mixing, coef], axis=0), v)
        bs[h] = bs[h] + both[:T]
        l_out[h] = both[T:].astype(BF16)

        @pl.when(h != k)
        def _():
            remote(l_out.at[h], l_in.at[k], l_send, l_recv.at[k], f, h).start()

        @pl.when(h == k)
        def _():
            l_in[h] = l_out[h]

    loop(heads + 1, head_local, 1)
    loop(shards, h_away)

    def carry_wait(j):
        g = ring(k, j, blocks)
        arrived(carry_in.at[g], k_recv.at[g])

    loop(blocks, carry_wait, 1)

    def chain(came, out, back, in_sem, send_sem, back_sem, backward):
        def link(i, state):
            b = blocks - 1 - i if backward else i
            out[b] = state.astype(BF16)

            @pl.when(b != k)
            def _():
                arrived(came.at[b], in_sem.at[b])

            return carry_in[b, 0:1, :] * state + came[b].astype(F32)

        lax.fori_loop(0, blocks, link, jnp.zeros((N, T), F32))

        def give(j):
            b = ring(k, j, blocks)
            remote(out.at[b], back.at[k], send_sem, back_sem.at[k], f, b).start()

        loop(blocks, give, 1)
        back[k] = out[k]

    chain(l_in, s_out, s_in, l_recv, s_send, s_recv, False)

    sg[...] = jnp.zeros_like(sg)
    acc_c[...] = jnp.zeros_like(acc_c)
    acc_b[...] = jnp.zeros_like(acc_b)

    def head_error(j):
        h = ring(k, heads - j, heads)

        @pl.when(h != k)
        def _():
            arrived(s_in.at[h], s_recv.at[h])

        v = val[:, lanes(h)]
        state = s_in[h]
        col = dcb[h]
        growth = jnp.exp(col)
        grown_state = growth * dot(map_c, state)
        err = bs[h] + grown_state
        grad = err * scale
        loss_s[pl.ds(h, 1), :] = jnp.sum(err * err, axis=0, keepdims=True)
        skip_s[pl.ds(h, 1), :] = jnp.sum(grad * v.astype(F32), axis=0, keepdims=True)
        mix_grad = ws[h] * dot_last(grad.astype(BF16), v)
        sg[...] += mix_grad
        turn = mix_grad * scores * (col - decay_s[pl.ds(h, 1), :]) + grad * grown_state * col
        alog_s[pl.ds(h, 1), :] = jnp.sum(turn, axis=0, keepdims=True)
        grown = (growth * grad).astype(BF16)
        e_out[h] = dot(map_c_t, grown).astype(BF16)
        acc_c[...] += dot_last(state, grown)

        @pl.when(h != k)
        def _():
            remote(e_out.at[h], e_in.at[k], e_send, e_recv.at[k], f, h).start()

        @pl.when(h == k)
        def _():
            e_in[h] = e_out[h]

    loop(heads + 1, head_error, 1)

    for hop in range(1, chips):
        j = ring(x, hop, chips) * 2 + c
        piece = hq.at[pl.ds(pl.multiple_of(j * T, T), T)]
        arrived(piece, h_recv.at[j])
        remote(piece, piece, h_fwd, h_recv.at[j], f, sib).start()

    chain(e_in, x_out, x_in, e_recv, x_send, x_recv, True)

    def head_exit(j):
        h = ring(k, heads - j, heads)

        @pl.when(h != k)
        def _():
            arrived(x_in.at[h], x_recv.at[h])

        leaving = x_in[h]
        last = fin_s[pl.ds(h, 1), :]
        weighed = dot_last(leaving, val[:, lanes(h)]) * we_s[pl.ds(h, 1), :]
        acc_b[...] += weighed
        end = jnp.sum(weighed * map_bt, axis=0, keepdims=True)
        kept = jnp.sum(leaving.astype(F32) * s_in[h].astype(F32), axis=0, keepdims=True)
        alog_s[pl.ds(h, 1), :] += end * (last - decay_s[pl.ds(h, 1), :]) + last * jnp.exp(last) * kept

    loop(heads + 1, head_exit, 1)

    score_bf = sg[...].astype(BF16)
    pg_out[0] = (dot(map_c_t, score_bf) + acc_b[...]).astype(BF16)
    pg_out[1] = (dot_last(map_b_t, score_bf) + acc_c[...]).astype(BF16)
    own_cols = lanes(o)

    def pg_go(j):
        there = ring(o, j, octet)
        remote(
            pg_out.at[lax.rem(there, 2)], pg_in.at[:, own_cols], p_send, p_recv.at[o], f, first + there
        ).start()

    loop(octet, pg_go, 1)
    pg_in[:, own_cols] = pg_out[c]

    lane = lax.broadcasted_iota(jnp.int32, (heads, T), 1)
    alog = jnp.sum(alog_s[...], axis=1, keepdims=True)
    skip = jnp.sum(skip_s[...], axis=1, keepdims=True)
    loss = jnp.sum(loss_s[...], axis=1, keepdims=True) * (0.5 * scale)
    c_out[...] = jnp.where(lane == 0, alog, jnp.where(lane == 1, skip, jnp.where(lane == 2, loss, 0.0)))

    def c_go(j):
        remote(c_out, c_in.at[f], c_send, c_recv.at[f], ring(f, j, shards), k).start()

    loop(shards, c_go, 1)
    c_in[f] = c_out[...]

    def h_wait(j):
        src = j * 2 + 1 - c
        arrived(hq.at[pl.ds(pl.multiple_of(src * T, T), T)], h_recv.at[src])

    loop(chips, h_wait)

    def pg_wait(j):
        src = ring(o, j, octet)
        arrived(pg_in.at[:, lanes(src)], p_recv.at[src])

    loop(octet, pg_wait, 1)

    def r_go(j):
        g = ring(f, j, shards)
        r_out[g] = dot(pg_in[...], hq[:, lanes(g)]).astype(BF16)

        @pl.when(g != f)
        def _():
            remote(r_out.at[g], r_in.at[f], r_send, r_recv.at[f], g, k).start()

        @pl.when(g == f)
        def _():
            r_in[g] = r_out[g]

    loop(shards + 1, r_go, 1)

    def r_wait(j):
        g = ring(f, j, shards)
        arrived(r_in.at[g], r_recv.at[g])
        arrived(c_in.at[g], c_recv.at[g])

    loop(shards, r_wait, 1)
    y_out[0:N, :] = lax.fori_loop(0, shards, lambda i, s: s + r_in[i].astype(F32), jnp.zeros((N, T), F32))
    y_out[N:, :] = lax.fori_loop(0, shards, lambda i, s: s + c_in[i], jnp.zeros((heads, T), F32))

    for hop in range(1, rows):
        remote(y_out, y_in.at[yh], y_send.at[hop], y_recv.at[yh], f, ring(yh, hop, rows) * octet + o).start()
    y_in[yh] = y_out[...]
    for hop in range(1, rows):
        src = ring(yh, hop, rows)
        arrived(y_in.at[src], y_recv.at[src])
    total = y_in[0]
    for i in range(1, rows):
        total = total + y_in[i]
    z_out[...] = total

    def z_go(j):
        remote(z_out, z_in.at[o], z_send, z_recv.at[o], f, first + ring(o, j, octet)).start()

    loop(octet, z_go, 1)
    z_in[o] = z_out[...]

    def z_wait(j):
        src = ring(o, j, octet)
        arrived(z_in.at[src], z_recv.at[src])

    loop(octet, z_wait, 1)
    for i in range(chips):
        ow[i * T : (i + 1) * T, :] = jnp.transpose(
            jnp.concatenate([z_in[2 * i, 0:N, :], z_in[2 * i + 1, 0:N, :]], axis=0)
        )
    sums = z_in[0, N:, :]
    for i in range(1, octet):
        sums = sums + z_in[i, N:, :]
    osc[...] = sums

    others = pl.ds(0, blocks - 1)
    peers = pl.ds(0, shards - 1)
    left(wbuf.at[peers, pl.ds(0, part)], w_send)
    left(wbuf.at[:, pl.ds(0, (chips - 1) * part)], v_send)
    left(wbuf.at[:, pl.ds(0, chips * part)], u_send)
    left(hq.at[pl.ds(0, min(2, chips - 1) * T)], h_send)
    if chips > 3:
        left(hq.at[pl.ds(0, (chips - 3) * T)], h_far)
    left(hq.at[pl.ds(0, T)], h_own)
    left(hq.at[pl.ds(0, (chips - 1) * T)], h_fwd)
    left(carry_out.at[others], k_send)
    left(l_out.at[others], l_send)
    left(s_out.at[others], s_send)
    left(e_out.at[others], e_send)
    left(x_out.at[others], x_send)
    left(pg_in.at[:, pl.ds(0, (octet - 1) * T)], p_send)
    left(r_out.at[peers], r_send)
    left(c_in.at[peers], c_send)
    for hop in range(1, rows):
        left(y_out, y_send.at[hop])
    left(z_in.at[pl.ds(0, octet - 1)], z_send)


def local(hidden, values, targets, dt_raw, proj_weight, a_log, skip):
    shards = lax.axis_size("fsdp")
    blocks = lax.axis_size("ctx")
    heads = a_log.shape[0]
    wide, both = proj_weight.shape
    octet = 2 * ROW_CHIPS
    rows = blocks // octet
    scale = 1.0 / (values.shape[2] * math.sqrt(shards * hidden.shape[1] * blocks))
    vmem = pltpu.VMEM
    per_head = lambda kind: vmem((heads, N, T), kind)
    small = vmem((heads, T), F32)
    one = pltpu.SemaphoreType.DMA
    many = lambda n: pltpu.SemaphoreType.DMA((n,))
    scratch = [
        vmem(hidden.shape[1:], BF16), vmem(values.shape[1:], BF16), vmem(targets.shape[1:], BF16),
        small, vmem((wide, both), BF16), many(5),
        vmem((shards, wide, both), BF16),
        vmem((octet * T, shards * T), BF16),
        vmem((heads, T, T), F32), vmem((heads, T, T), F32), vmem((heads, T, T), F32),
        *[small] * 8,
        vmem((heads, 8, T), F32), vmem((blocks, 8, T), F32),
        *[per_head(BF16)] * 8,
        vmem((T, T), F32), vmem((N, T), F32), vmem((N, T), F32),
        vmem((2, N, T), BF16), vmem((N, octet * T), BF16),
        vmem((shards, N, T), BF16), vmem((shards, N, T), BF16),
        small, vmem((shards, heads, T), F32),
        vmem((N + heads, T), F32), vmem((rows, N + heads, T), F32),
        vmem((N + heads, T), F32), vmem((octet, N + heads, T), F32),
        one, many(shards), one, many(octet), one, one, one, one, one, many(octet), one, many(blocks),
        *[one, many(blocks)] * 4,
        one, many(octet), one, many(shards), one, many(shards), many(rows), many(rows), one, many(octet),
    ]
    spec = pl.BlockSpec(memory_space=vmem)
    grad_w, sums = pl.pallas_call(
        functools.partial(body, shards, blocks, scale),
        out_shape=(
            jax.ShapeDtypeStruct((wide, both), F32),
            jax.ShapeDtypeStruct((heads, T), F32),
        ),
        in_specs=[pl.BlockSpec(memory_space=pltpu.HBM)] * 5 + [pl.BlockSpec(memory_space=pltpu.SMEM)] * 2,
        out_specs=(spec, spec),
        scratch_shapes=scratch,
        compiler_params=pltpu.CompilerParams(
            collective_id=0, has_side_effects=True, vmem_limit_bytes=56 * 2**20
        ),
    )(hidden[0], values[0], targets[0], dt_raw[0], proj_weight, a_log, skip)
    return (grad_w, sums[:, 0], sums[:, 1], jnp.sum(sums[:, 2]))


def solution(mesh):
    in_specs = (
        P("fsdp", "ctx", None),
        P("fsdp", "ctx", None),
        P("fsdp", "ctx", None),
        P("fsdp", None, "ctx"),
        P("fsdp", None),
        P(),
        P(),
    )
    out_specs = (P("fsdp", None), P(), P(), P())
    return jax.shard_map(local, mesh=mesh, in_specs=in_specs, out_specs=out_specs, check_vma=False)
```

```python
import functools
import math

import jax
import jax.numpy as jnp
from jax import lax
from jax.experimental import pallas as pl
from jax.experimental.pallas import tpu as pltpu
from jax.sharding import PartitionSpec as P

HIGHEST = lax.Precision.HIGHEST
MESH = pl.DeviceIdType.MESH
F32 = jnp.float32
BF16 = jnp.bfloat16
T = 128
N = 64
GROUP = 4
ROW_CHIPS = 4


def dot(left, right):
    return jnp.dot(left, right, preferred_element_type=F32)


def dot_last(left, right):
    return lax.dot_general(left, right, (((1,), (1,)), ((), ())), preferred_element_type=F32)


def body(
    shards, blocks, scale,
    hid_h, val_h, tgt_h, dt_h, w_h, a_ref, skip_ref, ow, osc,
    hid, val, tgt, dt, w, in_sem, wbuf, hq, ws, dcb, bs, rate_s, step_s, decay_s, fin_s, we_s, alog_s, skip_s, loss_s,
    fin_sib, early_s, late_s, carry_out, carry_in,
    l_out, l_sib, s_raw, s_pass, s_in, e_out, e_sib, x_raw, x_pass, x_in,
    l_pair, l_in, s_out, e_pair, e_in, x_out,
    sg, acc_c, acc_b, pg_out, pg_in, r_out, r_in, c_out, c_in, y_out, y_in, z_out, z_in, d_out, d_in, t_out, t_in,
    w_send, w_recv, v_send, v_recv, u_send, h_send, h_far, h_own, h_fwd, h_recv, n_send, n_recv, k_send, k_recv,
    l_send, l_recv, s_send, s_recv, e_send, e_recv, x_send, x_recv,
    lp_send, lp_recv, sp_send, sp_recv, ep_send, ep_recv, xp_send, xp_recv,
    p_send, p_recv, r_send, r_recv, c_send, c_recv, y_send, y_recv, z_send, z_recv,
    d_send, d_recv, t_send, t_recv,
):
    heads = dt.shape[0]
    wide = w.shape[0]
    part = wide // (2 * ROW_CHIPS)
    chips = ROW_CHIPS
    octet = 2 * chips
    rows = blocks // octet
    f = lax.axis_index("fsdp")
    k = lax.axis_index("ctx")
    c = lax.rem(k, 2)
    o = lax.rem(k, octet)
    yh = lax.div(k, octet)
    x = lax.div(o, 2)
    first = yh * octet
    sib = k + 1 - 2 * c
    pairs = blocks // 2
    q = lax.div(k, 2)

    def mine(p):
        return 2 * p + c

    def theirs(p):
        return 2 * p + 1 - c

    def by_core(own_first, own_second):
        return jnp.where(c == 0, own_first, own_second)


    def ring(start, hop, count):
        return lax.rem(start + hop, count)

    def remote(src, dst, ss, rs, to_f, to_k):
        return pltpu.make_async_remote_copy(
            src_ref=src, dst_ref=dst, send_sem=ss, recv_sem=rs,
            device_id=(to_f, to_k), device_id_type=MESH,
        )

    def arrived(dst, rs):
        remote(dst, dst, rs, rs, f, sib).wait_recv()

    def left(src, ss):
        remote(src, src, ss, ss, f, sib).wait_send()

    def loop(count, fn, start=0):
        def step(i, carry):
            fn(i)
            return carry

        lax.fori_loop(start, count, step, 0)

    def lanes(i):
        return pl.ds(pl.multiple_of(i * T, T), T)

    barrier = pltpu.get_barrier_semaphore()

    def greet_f(j):
        pl.semaphore_signal(barrier, inc=1, device_id=(ring(f, j, shards), k), device_id_type=MESH)

    def greet_k(j):
        pl.semaphore_signal(barrier, inc=1, device_id=(f, ring(k, j, blocks)), device_id_type=MESH)

    loop(shards, greet_f, 1)
    loop(blocks, greet_k, 1)
    loads = [
        pltpu.make_async_copy(src, dst, in_sem.at[i])
        for i, (src, dst) in enumerate(((w_h, w), (dt_h, dt), (val_h, val), (tgt_h, tgt), (hid_h, hid)))
    ]
    for load in loads:
        load.start()
    loads[0].wait()
    pl.semaphore_wait(barrier, shards + blocks - 2)

    own_part = pl.ds(pl.multiple_of(o * part, part), part)

    def w_go(j):
        remote(w.at[own_part], wbuf.at[f, own_part], w_send, w_recv.at[f], ring(f, j, shards), k).start()

    loop(shards, w_go, 1)
    wbuf[f, own_part, :] = w[own_part, :]

    loads[1].wait()

    def spread(h):
        rate_s[pl.ds(h, 1), :] = jnp.full((1, T), a_ref[h], F32)

    loop(heads, spread)
    step = jnp.maximum(dt[...], 0.0) + jnp.log1p(jnp.exp(-jnp.abs(dt[...])))
    row_id = lax.broadcasted_iota(jnp.int32, (T, T), 0)
    col_id = lax.broadcasted_iota(jnp.int32, (T, T), 1)
    upper = jnp.where(row_id <= col_id, 1.0, 0.0).astype(F32)
    decay = jnp.dot(-step * jnp.exp(rate_s[...]), upper, precision=HIGHEST, preferred_element_type=F32)
    fin = jnp.broadcast_to(decay[:, T - 1 :], (heads, T))
    step_s[...] = step
    decay_s[...] = decay
    fin_s[...] = fin
    we_s[...] = jnp.exp(fin - decay) * step

    remote(fin_s, fin_sib, n_send, n_recv, f, sib).start()

    def w_pass(j):
        g = ring(f, shards - j, shards)
        slot = wbuf.at[g, own_part]

        @pl.when(j > 0)
        def _():
            arrived(slot, w_recv.at[g])

        for hop in range(1, chips):
            there = first + ring(x, hop, chips) * 2 + c
            remote(slot, slot, v_send, v_recv.at[o], f, there).start()

    loop(shards, w_pass)
    own_slab = wbuf.at[:, own_part]
    remote(own_slab, own_slab, u_send, v_recv.at[o], f, sib).start()

    arrived(fin_sib, n_recv)
    early_s[...] = jnp.exp(by_core(fin_s[...], fin_sib[...]))
    late_s[...] = jnp.exp(by_core(fin_sib[...], fin_s[...]))

    def carry_go(p):
        h = mine(p)
        both = early_s[pl.ds(h, 1), :] * late_s[pl.ds(h, 1), :]
        carry_out[p] = jnp.broadcast_to(both, (8, T))

        @pl.when(p != q)
        def _():
            remote(carry_out.at[p], carry_in.at[q], k_send, k_recv.at[q], f, h).start()

        @pl.when(p == q)
        def _():
            carry_in[p] = carry_out[p]

    loop(pairs, carry_go)

    own_rows = pl.ds(pl.multiple_of(o * T, T), T)

    def hid_to(i, hop, sem):
        there = ring(x, hop, chips)
        remote(
            hid.at[:, pl.ds(pl.multiple_of(i * wide + there * T, T), T)], hq.at[own_rows, lanes(i)],
            sem, h_recv.at[o], f, first + there * 2 + c,
        ).start()

    loads[4].wait()

    def h_near(i):
        hid_to(i, 1, h_send)
        if chips > 2:
            hid_to(i, chips - 1, h_send)
        hq[own_rows, lanes(i)] = hid[:, pl.ds(pl.multiple_of(i * wide + x * T, T), T)]

    def h_away(i):
        for hop in range(2, chips - 1):
            hid_to(i, hop, h_far)

    loop(shards, h_near)
    remote(hq.at[own_rows], hq.at[own_rows], h_own, h_recv.at[o], f, sib).start()

    loads[2].wait()
    loads[3].wait()
    lower = row_id >= col_id

    def head_start(i):
        for u in range(GROUP):
            head_start_one(i * GROUP + u)

    def head_start_one(h):
        drow = decay_s[pl.ds(h, 1), :]
        col = jnp.transpose(jnp.broadcast_to(drow, (T, T)))
        dcb[h] = col
        within = jnp.where(lower, jnp.exp(jnp.minimum(col - drow, 0.0)), 0.0)
        ws[h] = within * step_s[pl.ds(h, 1), :]
        bs[h] = skip_ref[h] * val[:, lanes(h)].astype(F32) - tgt[:, lanes(h)].astype(F32)

    loop(heads // GROUP, head_start)

    def slab(src):
        return wbuf.at[:, pl.ds(pl.multiple_of(src * part, part), part)]

    for hop in range(1, chips):
        src = ring(x, hop, chips) * 2 + c
        arrived(slab(src), v_recv.at[src])
        remote(slab(src), slab(src), u_send, v_recv.at[src], f, sib).start()

    def w_rest(j):
        src = j * 2 + 1 - c
        arrived(slab(src), v_recv.at[src])

    loop(chips, w_rest)
    proj = dot(hid[...], wbuf[...].reshape(shards * wide, 2 * N))
    proj = proj.astype(BF16).astype(F32)
    proj_t = jnp.transpose(proj)
    map_bt = proj_t[:N]
    map_b_t = proj_t[:N].astype(BF16)
    map_c_t = proj_t[N:].astype(BF16)
    map_c = proj[:, N:].astype(BF16)
    scores = dot(map_c, map_b_t)

    def target(group, u):
        return ring(q, group * GROUP + u + 1, pairs)

    def origin(group, u):
        return ring(q, pairs - 1 - group * GROUP - u, pairs)

    def hand_over(p, out, come, send_sem, recv_sem):
        @pl.when(p != q)
        def _():
            remote(out.at[p], come.at[q], send_sem, recv_sem.at[q], f, mine(p)).start()

        @pl.when(p == q)
        def _():
            come[p] = out[p]

    def head_local_theirs(i):
        for u in range(GROUP):
            head_local_one(theirs(target(i, u)))
        for u in range(GROUP):
            h = theirs(target(i, u))
            remote(l_out.at[h], l_sib.at[h], lp_send, lp_recv.at[h], f, sib).start()

    def head_local_mine(i):
        for u in range(GROUP):
            head_local_one(mine(target(i, u)))
        for u in range(GROUP):
            p = target(i, u)
            h = mine(p)
            arrived(l_sib.at[h], lp_recv.at[h])
            own, other = l_out[h].astype(F32), l_sib[h].astype(F32)
            joined = late_s[pl.ds(h, 1), :] * by_core(own, other) + by_core(other, own)
            l_pair[p] = joined.astype(BF16)
            hand_over(p, l_pair, l_in, l_send, l_recv)

    def head_local_one(h):
        v = val[:, lanes(h)]
        mixing = (ws[h] * scores).astype(BF16)
        coef = (map_bt * we_s[pl.ds(h, 1), :]).astype(BF16)
        both = dot(jnp.concatenate([mixing, coef], axis=0), v)
        bs[h] = bs[h] + both[:T]
        l_out[h] = both[T:].astype(BF16)

    loop(pairs // GROUP, head_local_theirs)
    loop(pairs // GROUP, head_local_mine)
    loop(shards, h_away)

    def carry_wait(j):
        g = ring(q, j, pairs)
        arrived(carry_in.at[g], k_recv.at[g])

    loop(pairs, carry_wait, 1)

    def chain(came, out, back, in_sem, send_sem, back_sem, backward):
        def link(i, state):
            b = pairs - 1 - i if backward else i
            out[b] = state.astype(BF16)

            @pl.when(b != q)
            def _():
                arrived(came.at[b], in_sem.at[b])

            return carry_in[b, 0:1, :] * state + came[b].astype(F32)

        lax.fori_loop(0, pairs, link, jnp.zeros((N, T), F32))

        def give(j):
            b = ring(q, j, pairs)
            remote(out.at[b], back.at[k], send_sem, back_sem.at[k], f, mine(b)).start()

        loop(pairs, give, 1)
        back[k] = out[q]

    chain(l_in, s_out, s_raw, l_recv, s_send, s_recv, False)

    sg[...] = jnp.zeros_like(sg)
    acc_c[...] = jnp.zeros_like(acc_c)
    acc_b[...] = jnp.zeros_like(acc_b)

    def await_head(h, back, sem):
        @pl.when(h != k)
        def _():
            arrived(back.at[h], sem.at[h])

    def error_group(hs):
        parts = [head_error_one(h) for h in hs]
        sg[...] += sum(p[0] for p in parts)
        acc_c[...] += sum(p[1] for p in parts)

    def entries(i):
        for u in range(GROUP):
            p = origin(i, u)
            h = mine(p)
            arrived(e_sib.at[h], ep_recv.at[h])
            own, other = e_out[h].astype(F32), e_sib[h].astype(F32)
            joined = by_core(own, other) + early_s[pl.ds(h, 1), :] * by_core(other, own)
            e_pair[p] = joined.astype(BF16)
            hand_over(p, e_pair, e_in, e_send, e_recv)

    def head_error(i):
        hs = [mine(origin(i, u)) for u in range(GROUP)]
        for h in hs:
            await_head(h, s_raw, s_recv)
        for h in hs:
            state = s_raw[h].astype(F32)
            first_local = by_core(l_out[h], l_sib[h]).astype(F32)
            after = early_s[pl.ds(h, 1), :] * state + first_local
            s_in[h] = by_core(state, after).astype(BF16)
            s_pass[h] = by_core(after, state).astype(BF16)
            remote(s_pass.at[h], s_in.at[h], sp_send, sp_recv.at[h], f, sib).start()
        error_group(hs)

        @pl.when(i > 0)
        def _():
            entries(i - 1)

        hs = [theirs(origin(i, u)) for u in range(GROUP)]
        for h in hs:
            arrived(s_in.at[h], sp_recv.at[h])
        error_group(hs)
        for h in hs:
            remote(e_out.at[h], e_sib.at[h], ep_send, ep_recv.at[h], f, sib).start()

    def head_error_one(h):
        v = val[:, lanes(h)]
        state = s_in[h]
        col = dcb[h]
        growth = jnp.exp(col)
        grown_state = growth * dot(map_c, state)
        err = bs[h] + grown_state
        grad = err * scale
        loss_s[pl.ds(h, 1), :] = jnp.sum(err * err, axis=0, keepdims=True)
        skip_s[pl.ds(h, 1), :] = jnp.sum(grad * v.astype(F32), axis=0, keepdims=True)
        mix_grad = ws[h] * dot_last(grad.astype(BF16), v)
        turn = mix_grad * scores * (col - decay_s[pl.ds(h, 1), :]) + grad * grown_state * col
        alog_s[pl.ds(h, 1), :] = jnp.sum(turn, axis=0, keepdims=True)
        grown = (growth * grad).astype(BF16)
        e_out[h] = dot(map_c_t, grown).astype(BF16)
        return mix_grad, dot_last(state, grown)

    loop(pairs // GROUP, head_error)
    entries(pairs // GROUP - 1)

    for hop in range(1, chips):
        j = ring(x, hop, chips) * 2 + c
        piece = hq.at[pl.ds(pl.multiple_of(j * T, T), T)]
        arrived(piece, h_recv.at[j])
        remote(piece, piece, h_fwd, h_recv.at[j], f, sib).start()

    chain(e_in, x_out, x_raw, e_recv, x_send, x_recv, True)

    def head_exit(i):
        hs = [mine(origin(i, u)) for u in range(GROUP)]
        for h in hs:
            await_head(h, x_raw, x_recv)
        for h in hs:
            exit_late = x_raw[h].astype(F32)
            entry_late = by_core(e_sib[h], e_out[h]).astype(F32)
            exit_early = entry_late + late_s[pl.ds(h, 1), :] * exit_late
            x_in[h] = by_core(exit_early, exit_late).astype(BF16)
            x_pass[h] = by_core(exit_late, exit_early).astype(BF16)
            remote(x_pass.at[h], x_in.at[h], xp_send, xp_recv.at[h], f, sib).start()
        acc_b[...] += sum(head_exit_one(h) for h in hs)
        hs = [theirs(origin(i, u)) for u in range(GROUP)]
        for h in hs:
            arrived(x_in.at[h], xp_recv.at[h])
        acc_b[...] += sum(head_exit_one(h) for h in hs)

    def head_exit_one(h):
        leaving = x_in[h]
        last = fin_s[pl.ds(h, 1), :]
        weighed = dot_last(leaving, val[:, lanes(h)]) * we_s[pl.ds(h, 1), :]
        end = jnp.sum(weighed * map_bt, axis=0, keepdims=True)
        kept = jnp.sum(leaving.astype(F32) * s_in[h].astype(F32), axis=0, keepdims=True)
        alog_s[pl.ds(h, 1), :] += end * (last - decay_s[pl.ds(h, 1), :]) + last * jnp.exp(last) * kept
        return weighed

    loop(pairs // GROUP, head_exit)

    score_bf = sg[...].astype(BF16)
    pg_out[0] = (dot(map_c_t, score_bf) + acc_b[...]).astype(BF16)
    pg_out[1] = (dot_last(map_b_t, score_bf) + acc_c[...]).astype(BF16)
    own_cols = lanes(o)

    def pg_go(j):
        there = ring(o, j, octet)
        remote(
            pg_out.at[lax.rem(there, 2)], pg_in.at[:, own_cols], p_send, p_recv.at[o], f, first + there
        ).start()

    loop(octet, pg_go, 1)
    pg_in[:, own_cols] = pg_out[c]

    alog = jnp.sum(alog_s[...], axis=1, keepdims=True)
    skip = jnp.sum(skip_s[...], axis=1, keepdims=True)
    loss = jnp.sum(loss_s[...], axis=1, keepdims=True) * (0.5 * scale)
    lane = lax.broadcasted_iota(jnp.int32, (heads, T), 1)
    tile = jnp.where(lane == 0, alog, jnp.where(lane == 1, skip, jnp.where(lane == 2, loss, 0.0)))
    square = jnp.concatenate([tile, jnp.zeros((T - heads, T), F32)], axis=0)
    c_out[...] = jnp.transpose(square)[0:8]

    def c_go(j):
        remote(c_out, c_in.at[f], c_send, c_recv.at[f], ring(f, j, shards), k).start()

    loop(shards, c_go, 1)
    c_in[f] = c_out[...]

    def h_wait(j):
        src = j * 2 + 1 - c
        arrived(hq.at[pl.ds(pl.multiple_of(src * T, T), T)], h_recv.at[src])

    loop(chips, h_wait)

    def pg_wait(j):
        src = ring(o, j, octet)
        arrived(pg_in.at[:, lanes(src)], p_recv.at[src])

    loop(octet, pg_wait, 1)

    def r_go(j):
        g = ring(f, j, shards)
        r_out[g] = dot(pg_in[...], hq[:, lanes(g)]).astype(BF16)

        @pl.when(g != f)
        def _():
            remote(r_out.at[g], r_in.at[f], r_send, r_recv.at[f], g, k).start()

        @pl.when(g == f)
        def _():
            r_in[g] = r_out[g]

    loop(shards + 1, r_go, 1)

    def r_wait(j):
        g = ring(f, j, shards)
        arrived(r_in.at[g], r_recv.at[g])
        arrived(c_in.at[g], c_recv.at[g])

    loop(shards, r_wait, 1)
    total = r_in[0].astype(F32)
    sums = c_in[0]
    for i in range(1, shards):
        total = total + r_in[i].astype(F32)
        sums = sums + c_in[i]
    y_out[...] = total.astype(BF16)
    d_out[...] = sums

    for hop in range(1, rows):
        there = ring(yh, hop, rows) * octet + o
        remote(y_out, y_in.at[yh], y_send.at[hop], y_recv.at[yh], f, there).start()
        remote(d_out, d_in.at[yh], d_send.at[hop], d_recv.at[yh], f, there).start()
    y_in[yh] = y_out[...]
    d_in[yh] = d_out[...]
    for hop in range(1, rows):
        src = ring(yh, hop, rows)
        arrived(y_in.at[src], y_recv.at[src])
        arrived(d_in.at[src], d_recv.at[src])
    total = y_in[0].astype(F32)
    sums = d_in[0]
    for i in range(1, rows):
        total = total + y_in[i].astype(F32)
        sums = sums + d_in[i]
    z_out[...] = total.astype(BF16)
    t_out[...] = sums

    def z_go(j):
        there = first + ring(o, j, octet)
        remote(z_out, z_in.at[o], z_send, z_recv.at[o], f, there).start()
        remote(t_out, t_in.at[o], t_send, t_recv.at[o], f, there).start()

    loop(octet, z_go, 1)
    z_in[o] = z_out[...]
    t_in[o] = t_out[...]

    def z_wait(j):
        src = ring(o, j, octet)
        arrived(z_in.at[src], z_recv.at[src])
        arrived(t_in.at[src], t_recv.at[src])

    loop(octet, z_wait, 1)
    for i in range(chips):
        ow[i * T : (i + 1) * T, :] = jnp.transpose(
            jnp.concatenate([z_in[2 * i], z_in[2 * i + 1]], axis=0).astype(F32)
        )
    sums = t_in[0]
    for i in range(1, octet):
        sums = sums + t_in[i]
    osc[...] = sums

    others = pl.ds(0, pairs - 1)
    every = pl.ds(0, pairs)
    peers = pl.ds(0, shards - 1)
    left(wbuf.at[peers, pl.ds(0, part)], w_send)
    left(wbuf.at[:, pl.ds(0, (chips - 1) * part)], v_send)
    left(wbuf.at[:, pl.ds(0, chips * part)], u_send)
    left(hq.at[pl.ds(0, min(2, chips - 1) * T)], h_send)
    if chips > 3:
        left(hq.at[pl.ds(0, (chips - 3) * T)], h_far)
    left(hq.at[pl.ds(0, T)], h_own)
    left(hq.at[pl.ds(0, (chips - 1) * T)], h_fwd)
    left(carry_out.at[others], k_send)
    left(fin_s, n_send)
    left(l_pair.at[others], l_send)
    left(s_out.at[others], s_send)
    left(e_pair.at[others], e_send)
    left(x_out.at[others], x_send)
    left(l_out.at[every], lp_send)
    left(s_pass.at[every], sp_send)
    left(e_out.at[every], ep_send)
    left(x_pass.at[every], xp_send)
    left(pg_in.at[:, pl.ds(0, (octet - 1) * T)], p_send)
    left(r_out.at[peers], r_send)
    left(c_in.at[peers], c_send)
    for hop in range(1, rows):
        left(y_out, y_send.at[hop])
        left(d_out, d_send.at[hop])
    left(z_in.at[pl.ds(0, octet - 1)], z_send)
    left(t_in.at[pl.ds(0, octet - 1)], t_send)


def local(hidden, values, targets, dt_raw, proj_weight, a_log, skip):
    shards = lax.axis_size("fsdp")
    blocks = lax.axis_size("ctx")
    heads = a_log.shape[0]
    wide, both = proj_weight.shape
    octet = 2 * ROW_CHIPS
    rows = blocks // octet
    scale = 1.0 / (values.shape[2] * math.sqrt(shards * hidden.shape[1] * blocks))
    vmem = pltpu.VMEM
    per_head = lambda kind: vmem((heads, N, T), kind)
    small = vmem((heads, T), F32)
    one = pltpu.SemaphoreType.DMA
    many = lambda n: pltpu.SemaphoreType.DMA((n,))
    scratch = [
        vmem(hidden.shape[1:], BF16), vmem(values.shape[1:], BF16), vmem(targets.shape[1:], BF16),
        small, vmem((wide, both), BF16), many(5),
        vmem((shards, wide, both), BF16),
        vmem((octet * T, shards * T), BF16),
        vmem((heads, T, T), F32), vmem((heads, T, T), F32), vmem((heads, T, T), F32),
        *[small] * 8,
        small, small, small, vmem((blocks // 2, 8, T), F32), vmem((blocks // 2, 8, T), F32),
        *[per_head(BF16)] * 10,
        *[vmem((blocks // 2, N, T), BF16)] * 6,
        vmem((T, T), F32), vmem((N, T), F32), vmem((N, T), F32),
        vmem((2, N, T), BF16), vmem((N, octet * T), BF16),
        vmem((shards, N, T), BF16), vmem((shards, N, T), BF16),
        vmem((8, T), F32), vmem((shards, 8, T), F32),
        vmem((N, T), BF16), vmem((rows, N, T), BF16),
        vmem((N, T), BF16), vmem((octet, N, T), BF16),
        vmem((8, T), F32), vmem((rows, 8, T), F32), vmem((8, T), F32), vmem((octet, 8, T), F32),
        one, many(shards), one, many(octet), one, one, one, one, one, many(octet), one, one, one, many(blocks),
        *[one, many(blocks)] * 8,
        one, many(octet), one, many(shards), one, many(shards), many(rows), many(rows), one, many(octet),
        many(rows), many(rows), one, many(octet),
    ]
    spec = pl.BlockSpec(memory_space=vmem)
    grad_w, sums = pl.pallas_call(
        functools.partial(body, shards, blocks, scale),
        out_shape=(
            jax.ShapeDtypeStruct((wide, both), F32),
            jax.ShapeDtypeStruct((8, T), F32),
        ),
        in_specs=[pl.BlockSpec(memory_space=pltpu.HBM)] * 5 + [pl.BlockSpec(memory_space=pltpu.SMEM)] * 2,
        out_specs=(spec, spec),
        scratch_shapes=scratch,
        compiler_params=pltpu.CompilerParams(
            collective_id=0, has_side_effects=True, vmem_limit_bytes=56 * 2**20
        ),
    )(hidden[0], values[0], targets[0], dt_raw[0], proj_weight, a_log, skip)
    return (grad_w, sums[0, :heads], sums[1, :heads], jnp.sum(sums[2, :heads]))


def solution(mesh):
    in_specs = (
        P("fsdp", "ctx", None),
        P("fsdp", "ctx", None),
        P("fsdp", "ctx", None),
        P("fsdp", None, "ctx"),
        P("fsdp", None),
        P(),
        P(),
    )
    out_specs = (P("fsdp", None), P(), P(), P())
    return jax.shard_map(local, mesh=mesh, in_specs=in_specs, out_specs=out_specs, check_vma=False)
```

```python
import functools
import math

import jax
import jax.numpy as jnp
from jax import lax
from jax.experimental import pallas as pl
from jax.experimental.pallas import tpu as pltpu
from jax.sharding import PartitionSpec as P

HIGHEST = lax.Precision.HIGHEST
MESH = pl.DeviceIdType.MESH
F32 = jnp.float32
BF16 = jnp.bfloat16
T = 128
N = 64
GROUP = 4
ROW_CHIPS = 4


def dot(left, right):
    return jnp.dot(left, right, preferred_element_type=F32)


def dot_last(left, right):
    return lax.dot_general(left, right, (((1,), (1,)), ((), ())), preferred_element_type=F32)


def body(
    shards, blocks, scale,
    hid_h, val_h, tgt_h, dt_h, w_h, a_ref, skip_ref, ow, osc,
    hid, val, tgt, dt, in_sem, wbuf, hq, ws, dcb, bs, rate_s, step_s, decay_s, fin_s, we_s, alog_s, skip_s, loss_s,
    fin_sib, early_s, late_s, carry_out, carry_in,
    l_out, l_sib, s_raw, s_pass, s_in, e_out, e_sib, x_raw, x_pass, x_in,
    l_pair, l_in, s_out, e_pair, e_in, x_out,
    sg, acc_c, acc_b, pg_out, pg_in, r_out, r_in, c_out, c_in, y_out, y_in, z_out, z_in, d_out, d_in, t_out, t_in,
    w_send, w_recv, v_send, v_recv, u_send, h_send, h_fwd, h_recv, n_send, n_recv, k_send, k_recv,
    l_send, l_recv, s_send, s_recv, e_send, e_recv, x_send, x_recv,
    lp_send, lp_recv, sp_send, sp_recv, ep_send, ep_recv, xp_send, xp_recv,
    p_send, p_recv, r_send, r_recv, c_send, c_recv, y_send, y_recv, z_send, z_recv,
    d_send, d_recv, t_send, t_recv,
):
    heads = dt.shape[0]
    wide = w_h.shape[0]
    part = wide // (2 * ROW_CHIPS)
    chips = ROW_CHIPS
    octet = 2 * chips
    rows = blocks // octet
    f = lax.axis_index("fsdp")
    k = lax.axis_index("ctx")
    c = lax.rem(k, 2)
    o = lax.rem(k, octet)
    yh = lax.div(k, octet)
    x = lax.div(o, 2)
    first = yh * octet
    sib = k + 1 - 2 * c
    pairs = blocks // 2
    q = lax.div(k, 2)

    def mine(p):
        return 2 * p + c

    def theirs(p):
        return 2 * p + 1 - c

    def by_core(own_first, own_second):
        return jnp.where(c == 0, own_first, own_second)


    def ring(start, hop, count):
        return lax.rem(start + hop, count)

    def remote(src, dst, ss, rs, to_f, to_k):
        return pltpu.make_async_remote_copy(
            src_ref=src, dst_ref=dst, send_sem=ss, recv_sem=rs,
            device_id=(to_f, to_k), device_id_type=MESH,
        )

    def arrived(dst, rs):
        remote(dst, dst, rs, rs, f, sib).wait_recv()

    def left(src, ss):
        remote(src, src, ss, ss, f, sib).wait_send()

    def loop(count, fn, start=0):
        def step(i, carry):
            fn(i)
            return carry

        lax.fori_loop(start, count, step, 0)

    def lanes(i):
        return pl.ds(pl.multiple_of(i * T, T), T)

    barrier = pltpu.get_barrier_semaphore()

    def greet_f(j):
        pl.semaphore_signal(barrier, inc=1, device_id=(ring(f, j, shards), k), device_id_type=MESH)

    def greet_k(j):
        pl.semaphore_signal(barrier, inc=1, device_id=(f, ring(k, j, blocks)), device_id_type=MESH)

    loop(shards, greet_f, 1)
    loop(blocks, greet_k, 1)
    loads = [
        pltpu.make_async_copy(src, dst, in_sem.at[i])
        for i, (src, dst) in enumerate(((dt_h, dt), (val_h, val), (tgt_h, tgt), (hid_h, hid)), 1)
    ]
    for load in loads:
        load.start()
    pl.semaphore_wait(barrier, shards + blocks - 2)

    own_part = pl.ds(pl.multiple_of(o * part, part), part)

    def w_go(j):
        remote(w_h.at[own_part], wbuf.at[f, own_part], w_send, w_recv.at[f], ring(f, j, shards), k).start()

    loop(shards, w_go, 1)
    own_copy = pltpu.make_async_copy(w_h.at[own_part], wbuf.at[f, own_part], in_sem.at[0])
    own_copy.start()

    loads[0].wait()

    def spread(h):
        rate_s[pl.ds(h, 1), :] = jnp.full((1, T), a_ref[h], F32)

    loop(heads, spread)
    step = jnp.maximum(dt[...], 0.0) + jnp.log1p(jnp.exp(-jnp.abs(dt[...])))
    row_id = lax.broadcasted_iota(jnp.int32, (T, T), 0)
    col_id = lax.broadcasted_iota(jnp.int32, (T, T), 1)
    upper = jnp.where(row_id <= col_id, 1.0, 0.0).astype(F32)
    decay = jnp.dot(-step * jnp.exp(rate_s[...]), upper, precision=HIGHEST, preferred_element_type=F32)
    fin = jnp.broadcast_to(decay[:, T - 1 :], (heads, T))
    step_s[...] = step
    decay_s[...] = decay
    fin_s[...] = fin
    we_s[...] = jnp.exp(fin - decay) * step

    remote(fin_s, fin_sib, n_send, n_recv, f, sib).start()

    def w_pass(j):
        g = ring(f, shards - j, shards)
        slot = wbuf.at[g, own_part]

        @pl.when(j > 0)
        def _():
            arrived(slot, w_recv.at[g])

        for hop in range(1, chips):
            there = first + ring(x, hop, chips) * 2 + c
            remote(slot, slot, v_send, v_recv.at[o], f, there).start()

    own_copy.wait()
    loop(shards, w_pass)
    own_slab = wbuf.at[:, own_part]
    remote(own_slab, own_slab, u_send, v_recv.at[o], f, sib).start()

    arrived(fin_sib, n_recv)
    early_s[...] = jnp.exp(by_core(fin_s[...], fin_sib[...]))
    late_s[...] = jnp.exp(by_core(fin_sib[...], fin_s[...]))

    def carry_go(p):
        h = mine(p)
        both = early_s[pl.ds(h, 1), :] * late_s[pl.ds(h, 1), :]
        carry_out[p] = jnp.broadcast_to(both, (8, T))

        @pl.when(p != q)
        def _():
            remote(carry_out.at[p], carry_in.at[q], k_send, k_recv.at[q], f, h).start()

        @pl.when(p == q)
        def _():
            carry_in[p] = carry_out[p]

    loop(pairs, carry_go)

    own_rows = pl.ds(pl.multiple_of(o * T, T), T)

    near_end, mid_end = shards * 3 // 8, shards * 3 // 4

    def h_go(i):
        part = jnp.where(i < mid_end, 0, octet)
        for hop in range(1, chips):
            there = ring(x, hop, chips)
            remote(
                hid.at[:, pl.ds(pl.multiple_of(i * wide + there * T, T), T)], hq.at[own_rows, lanes(i)],
                h_send, h_recv.at[part + o], f, first + there * 2 + c,
            ).start()

    def h_keep(i):
        hq[own_rows, lanes(i)] = hid[:, pl.ds(pl.multiple_of(i * wide + x * T, T), T)]

    def h_slab(src, late):
        start, size = (mid_end, shards - mid_end) if late else (0, mid_end)
        return hq.at[pl.ds(pl.multiple_of(src * T, T), T), pl.ds(start * T, size * T)]

    def h_next(src, late):
        there = h_recv.at[src + (octet if late else 0)]
        remote(h_slab(src, late), h_slab(src, late), h_fwd, there, f, sib).start()

    def h_pass(late):
        for hop in range(1, chips):
            src = ring(x, hop, chips) * 2 + c
            arrived(h_slab(src, late), h_recv.at[src + (octet if late else 0)])
            h_next(src, late)

    loads[3].wait()
    loop(near_end, h_go)
    loop(shards, h_keep)
    h_next(o, False)
    h_next(o, True)

    loads[1].wait()
    loads[2].wait()
    lower = row_id >= col_id

    def head_start(i):
        for u in range(GROUP):
            head_start_one(i * GROUP + u)

    def head_start_one(h):
        drow = decay_s[pl.ds(h, 1), :]
        col = jnp.transpose(jnp.broadcast_to(drow, (T, T)))
        dcb[h] = col
        within = jnp.where(lower, jnp.exp(jnp.minimum(col - drow, 0.0)), 0.0)
        ws[h] = within * step_s[pl.ds(h, 1), :]
        bs[h] = skip_ref[h] * val[:, lanes(h)].astype(F32) - tgt[:, lanes(h)].astype(F32)

    loop(heads // GROUP, head_start)

    def slab(src):
        return wbuf.at[:, pl.ds(pl.multiple_of(src * part, part), part)]

    for hop in range(1, chips):
        src = ring(x, hop, chips) * 2 + c
        arrived(slab(src), v_recv.at[src])
        remote(slab(src), slab(src), u_send, v_recv.at[src], f, sib).start()

    def w_rest(j):
        src = j * 2 + 1 - c
        arrived(slab(src), v_recv.at[src])

    loop(chips, w_rest)
    proj = dot(hid[...], wbuf[...].reshape(shards * wide, 2 * N))
    proj = proj.astype(BF16).astype(F32)
    proj_t = jnp.transpose(proj)
    map_bt = proj_t[:N]
    map_b_t = proj_t[:N].astype(BF16)
    map_c_t = proj_t[N:].astype(BF16)
    map_c = proj[:, N:].astype(BF16)
    scores = dot(map_c, map_b_t)

    def target(group, u):
        return ring(q, group * GROUP + u + 1, pairs)

    def origin(group, u):
        return ring(q, pairs - 1 - group * GROUP - u, pairs)

    def hand_over(p, out, come, send_sem, recv_sem):
        @pl.when(p != q)
        def _():
            remote(out.at[p], come.at[q], send_sem, recv_sem.at[q], f, mine(p)).start()

        @pl.when(p == q)
        def _():
            come[p] = out[p]

    def head_local_theirs(i):
        for u in range(GROUP):
            head_local_one(theirs(target(i, u)))
        for u in range(GROUP):
            h = theirs(target(i, u))
            remote(l_out.at[h], l_sib.at[h], lp_send, lp_recv.at[h], f, sib).start()

    def head_local_mine(i):
        for u in range(GROUP):
            head_local_one(mine(target(i, u)))
        for u in range(GROUP):
            p = target(i, u)
            h = mine(p)
            arrived(l_sib.at[h], lp_recv.at[h])
            own, other = l_out[h].astype(F32), l_sib[h].astype(F32)
            joined = late_s[pl.ds(h, 1), :] * by_core(own, other) + by_core(other, own)
            l_pair[p] = joined.astype(BF16)
            hand_over(p, l_pair, l_in, l_send, l_recv)

    def head_local_one(h):
        v = val[:, lanes(h)]
        mixing = (ws[h] * scores).astype(BF16)
        coef = (map_bt * we_s[pl.ds(h, 1), :]).astype(BF16)
        both = dot(jnp.concatenate([mixing, coef], axis=0), v)
        bs[h] = bs[h] + both[:T]
        l_out[h] = both[T:].astype(BF16)

    loop(pairs // GROUP, head_local_theirs)
    loop(pairs // GROUP, head_local_mine)

    def carry_wait(j):
        g = ring(q, j, pairs)
        arrived(carry_in.at[g], k_recv.at[g])

    loop(pairs, carry_wait, 1)

    def chain(came, out, back, in_sem, send_sem, back_sem, backward):
        def link(i, state):
            b = pairs - 1 - i if backward else i
            out[b] = state.astype(BF16)

            @pl.when(b != q)
            def _():
                arrived(came.at[b], in_sem.at[b])

            return carry_in[b, 0:1, :] * state + came[b].astype(F32)

        lax.fori_loop(0, pairs, link, jnp.zeros((N, T), F32))

        def give(j):
            b = ring(q, j, pairs)
            remote(out.at[b], back.at[k], send_sem, back_sem.at[k], f, mine(b)).start()

        loop(pairs, give, 1)
        back[k] = out[q]

    chain(l_in, s_out, s_raw, l_recv, s_send, s_recv, False)
    loop(mid_end, h_go, near_end)

    sg[...] = jnp.zeros_like(sg)
    acc_c[...] = jnp.zeros_like(acc_c)
    acc_b[...] = jnp.zeros_like(acc_b)

    def await_head(h, back, sem):
        @pl.when(h != k)
        def _():
            arrived(back.at[h], sem.at[h])

    def error_group(hs):
        parts = [head_error_one(h) for h in hs]
        sg[...] += sum(p[0] for p in parts)
        acc_c[...] += sum(p[1] for p in parts)

    def entries(i):
        for u in range(GROUP):
            p = origin(i, u)
            h = mine(p)
            arrived(e_sib.at[h], ep_recv.at[h])
            own, other = e_out[h].astype(F32), e_sib[h].astype(F32)
            joined = by_core(own, other) + early_s[pl.ds(h, 1), :] * by_core(other, own)
            e_pair[p] = joined.astype(BF16)
            hand_over(p, e_pair, e_in, e_send, e_recv)

    def head_error(i):
        hs = [mine(origin(i, u)) for u in range(GROUP)]
        for h in hs:
            await_head(h, s_raw, s_recv)
        for h in hs:
            state = s_raw[h].astype(F32)
            first_local = by_core(l_out[h], l_sib[h]).astype(F32)
            after = early_s[pl.ds(h, 1), :] * state + first_local
            s_in[h] = by_core(state, after).astype(BF16)
            s_pass[h] = by_core(after, state).astype(BF16)
            remote(s_pass.at[h], s_in.at[h], sp_send, sp_recv.at[h], f, sib).start()
        error_group(hs)

        @pl.when(i > 0)
        def _():
            entries(i - 1)

        hs = [theirs(origin(i, u)) for u in range(GROUP)]
        for h in hs:
            arrived(s_in.at[h], sp_recv.at[h])
        error_group(hs)
        for h in hs:
            remote(e_out.at[h], e_sib.at[h], ep_send, ep_recv.at[h], f, sib).start()

    def head_error_one(h):
        v = val[:, lanes(h)]
        state = s_in[h]
        col = dcb[h]
        growth = jnp.exp(col)
        grown_state = growth * dot(map_c, state)
        err = bs[h] + grown_state
        grad = err * scale
        loss_s[pl.ds(h, 1), :] = jnp.sum(err * err, axis=0, keepdims=True)
        skip_s[pl.ds(h, 1), :] = jnp.sum(grad * v.astype(F32), axis=0, keepdims=True)
        mix_grad = ws[h] * dot_last(grad.astype(BF16), v)
        turn = mix_grad * scores * (col - decay_s[pl.ds(h, 1), :]) + grad * grown_state * col
        alog_s[pl.ds(h, 1), :] = jnp.sum(turn, axis=0, keepdims=True)
        grown = (growth * grad).astype(BF16)
        e_out[h] = dot(map_c_t, grown).astype(BF16)
        return mix_grad, dot_last(state, grown)

    loop(pairs // GROUP, head_error)
    entries(pairs // GROUP - 1)

    h_pass(False)

    chain(e_in, x_out, x_raw, e_recv, x_send, x_recv, True)
    loop(shards, h_go, mid_end)

    def head_exit(i):
        hs = [mine(origin(i, u)) for u in range(GROUP)]
        for h in hs:
            await_head(h, x_raw, x_recv)
        for h in hs:
            exit_late = x_raw[h].astype(F32)
            entry_late = by_core(e_sib[h], e_out[h]).astype(F32)
            exit_early = entry_late + late_s[pl.ds(h, 1), :] * exit_late
            x_in[h] = by_core(exit_early, exit_late).astype(BF16)
            x_pass[h] = by_core(exit_late, exit_early).astype(BF16)
            remote(x_pass.at[h], x_in.at[h], xp_send, xp_recv.at[h], f, sib).start()
        acc_b[...] += sum(head_exit_one(h) for h in hs)
        hs = [theirs(origin(i, u)) for u in range(GROUP)]
        for h in hs:
            arrived(x_in.at[h], xp_recv.at[h])
        acc_b[...] += sum(head_exit_one(h) for h in hs)

    def head_exit_one(h):
        leaving = x_in[h]
        last = fin_s[pl.ds(h, 1), :]
        weighed = dot_last(leaving, val[:, lanes(h)]) * we_s[pl.ds(h, 1), :]
        end = jnp.sum(weighed * map_bt, axis=0, keepdims=True)
        kept = jnp.sum(leaving.astype(F32) * s_in[h].astype(F32), axis=0, keepdims=True)
        alog_s[pl.ds(h, 1), :] += end * (last - decay_s[pl.ds(h, 1), :]) + last * jnp.exp(last) * kept
        return weighed

    loop(pairs // GROUP, head_exit)

    score_bf = sg[...].astype(BF16)
    pg_out[0] = (dot(map_c_t, score_bf) + acc_b[...]).astype(BF16)
    pg_out[1] = (dot_last(map_b_t, score_bf) + acc_c[...]).astype(BF16)
    own_cols = lanes(o)

    def pg_go(j):
        there = ring(o, j, octet)
        remote(
            pg_out.at[lax.rem(there, 2)], pg_in.at[:, own_cols], p_send, p_recv.at[o], f, first + there
        ).start()

    loop(octet, pg_go, 1)
    pg_in[:, own_cols] = pg_out[c]

    alog = jnp.sum(alog_s[...], axis=1, keepdims=True)
    skip = jnp.sum(skip_s[...], axis=1, keepdims=True)
    loss = jnp.sum(loss_s[...], axis=1, keepdims=True) * (0.5 * scale)
    lane = lax.broadcasted_iota(jnp.int32, (heads, T), 1)
    tile = jnp.where(lane == 0, alog, jnp.where(lane == 1, skip, jnp.where(lane == 2, loss, 0.0)))
    square = jnp.concatenate([tile, jnp.zeros((T - heads, T), F32)], axis=0)
    c_out[...] = jnp.transpose(square)[0:8]

    def c_go(j):
        remote(c_out, c_in.at[f], c_send, c_recv.at[f], ring(f, j, shards), k).start()

    loop(shards, c_go, 1)
    c_in[f] = c_out[...]

    h_pass(True)

    def h_wait(j):
        src = j * 2 + 1 - c
        arrived(h_slab(src, False), h_recv.at[src])
        arrived(h_slab(src, True), h_recv.at[octet + src])

    loop(chips, h_wait)

    def pg_wait(j):
        src = ring(o, j, octet)
        arrived(pg_in.at[:, lanes(src)], p_recv.at[src])

    loop(octet, pg_wait, 1)

    def r_go(j):
        two = ring(lax.div(f, 2), j, shards // 2)
        product = dot(pg_in[...], hq[:, pl.ds(pl.multiple_of(two * 2 * T, 2 * T), 2 * T)]).astype(BF16)
        for u in range(2):
            g = two * 2 + u
            r_out[g] = product[:, u * T : (u + 1) * T]

            @pl.when(g != f)
            def _():
                remote(r_out.at[g], r_in.at[f], r_send, r_recv.at[f], g, k).start()

            @pl.when(g == f)
            def _():
                r_in[g] = r_out[g]

    loop(shards // 2 + 1, r_go, 1)

    def r_wait(j):
        g = ring(f, j, shards)
        arrived(r_in.at[g], r_recv.at[g])
        arrived(c_in.at[g], c_recv.at[g])

    loop(shards, r_wait, 1)
    total = r_in[0].astype(F32)
    sums = c_in[0]
    for i in range(1, shards):
        total = total + r_in[i].astype(F32)
        sums = sums + c_in[i]
    y_out[...] = total.astype(BF16)
    d_out[...] = sums

    for hop in range(1, rows):
        there = ring(yh, hop, rows) * octet + o
        remote(y_out, y_in.at[yh], y_send.at[hop], y_recv.at[yh], f, there).start()
        remote(d_out, d_in.at[yh], d_send.at[hop], d_recv.at[yh], f, there).start()
    y_in[yh] = y_out[...]
    d_in[yh] = d_out[...]
    for hop in range(1, rows):
        src = ring(yh, hop, rows)
        arrived(y_in.at[src], y_recv.at[src])
        arrived(d_in.at[src], d_recv.at[src])
    total = y_in[0].astype(F32)
    sums = d_in[0]
    for i in range(1, rows):
        total = total + y_in[i].astype(F32)
        sums = sums + d_in[i]
    z_out[...] = total.astype(BF16)
    t_out[...] = sums

    def z_go(j):
        there = first + ring(o, j, octet)
        remote(z_out, z_in.at[o], z_send, z_recv.at[o], f, there).start()
        remote(t_out, t_in.at[o], t_send, t_recv.at[o], f, there).start()

    loop(octet, z_go, 1)
    z_in[o] = z_out[...]
    t_in[o] = t_out[...]

    def z_wait(j):
        src = ring(o, j, octet)
        arrived(z_in.at[src], z_recv.at[src])
        arrived(t_in.at[src], t_recv.at[src])

    loop(octet, z_wait, 1)
    for i in range(chips):
        ow[i * T : (i + 1) * T, :] = jnp.transpose(
            jnp.concatenate([z_in[2 * i], z_in[2 * i + 1]], axis=0).astype(F32)
        )
    sums = t_in[0]
    for i in range(1, octet):
        sums = sums + t_in[i]
    osc[...] = sums

    others = pl.ds(0, pairs - 1)
    every = pl.ds(0, pairs)
    peers = pl.ds(0, shards - 1)
    left(wbuf.at[peers, pl.ds(0, part)], w_send)
    left(wbuf.at[:, pl.ds(0, (chips - 1) * part)], v_send)
    left(wbuf.at[:, pl.ds(0, chips * part)], u_send)
    left(hq.at[pl.ds(0, (chips - 1) * T)], h_send)
    left(hq.at[pl.ds(0, chips * T)], h_fwd)
    left(carry_out.at[others], k_send)
    left(fin_s, n_send)
    left(l_pair.at[others], l_send)
    left(s_out.at[others], s_send)
    left(e_pair.at[others], e_send)
    left(x_out.at[others], x_send)
    left(l_out.at[every], lp_send)
    left(s_pass.at[every], sp_send)
    left(e_out.at[every], ep_send)
    left(x_pass.at[every], xp_send)
    left(pg_in.at[:, pl.ds(0, (octet - 1) * T)], p_send)
    left(r_out.at[peers], r_send)
    left(c_in.at[peers], c_send)
    for hop in range(1, rows):
        left(y_out, y_send.at[hop])
        left(d_out, d_send.at[hop])
    left(z_in.at[pl.ds(0, octet - 1)], z_send)
    left(t_in.at[pl.ds(0, octet - 1)], t_send)


def local(hidden, values, targets, dt_raw, proj_weight, a_log, skip):
    shards = lax.axis_size("fsdp")
    blocks = lax.axis_size("ctx")
    heads = a_log.shape[0]
    wide, both = proj_weight.shape
    octet = 2 * ROW_CHIPS
    rows = blocks // octet
    scale = 1.0 / (values.shape[2] * math.sqrt(shards * hidden.shape[1] * blocks))
    vmem = pltpu.VMEM
    per_head = lambda kind: vmem((heads, N, T), kind)
    small = vmem((heads, T), F32)
    one = pltpu.SemaphoreType.DMA
    many = lambda n: pltpu.SemaphoreType.DMA((n,))
    scratch = [
        vmem(hidden.shape[1:], BF16), vmem(values.shape[1:], BF16), vmem(targets.shape[1:], BF16),
        small, many(5),
        vmem((shards, wide, both), BF16),
        vmem((octet * T, shards * T), BF16),
        vmem((heads, T, T), F32), vmem((heads, T, T), F32), vmem((heads, T, T), F32),
        *[small] * 8,
        small, small, small, vmem((blocks // 2, 8, T), F32), vmem((blocks // 2, 8, T), F32),
        *[per_head(BF16)] * 10,
        *[vmem((blocks // 2, N, T), BF16)] * 6,
        vmem((T, T), F32), vmem((N, T), F32), vmem((N, T), F32),
        vmem((2, N, T), BF16), vmem((N, octet * T), BF16),
        vmem((shards, N, T), BF16), vmem((shards, N, T), BF16),
        vmem((8, T), F32), vmem((shards, 8, T), F32),
        vmem((N, T), BF16), vmem((rows, N, T), BF16),
        vmem((N, T), BF16), vmem((octet, N, T), BF16),
        vmem((8, T), F32), vmem((rows, 8, T), F32), vmem((8, T), F32), vmem((octet, 8, T), F32),
        one, many(shards), one, many(octet), one, one, one, many(2 * octet), one, one, one, many(blocks),
        *[one, many(blocks)] * 8,
        one, many(octet), one, many(shards), one, many(shards), many(rows), many(rows), one, many(octet),
        many(rows), many(rows), one, many(octet),
    ]
    spec = pl.BlockSpec(memory_space=vmem)
    grad_w, sums = pl.pallas_call(
        functools.partial(body, shards, blocks, scale),
        out_shape=(
            jax.ShapeDtypeStruct((wide, both), F32),
            jax.ShapeDtypeStruct((8, T), F32),
        ),
        in_specs=[pl.BlockSpec(memory_space=pltpu.HBM)] * 5 + [pl.BlockSpec(memory_space=pltpu.SMEM)] * 2,
        out_specs=(spec, spec),
        scratch_shapes=scratch,
        compiler_params=pltpu.CompilerParams(
            collective_id=0, has_side_effects=True, vmem_limit_bytes=56 * 2**20
        ),
    )(hidden[0], values[0], targets[0], dt_raw[0], proj_weight, a_log, skip)
    return (grad_w, sums[0, :heads], sums[1, :heads], jnp.sum(sums[2, :heads]))


def solution(mesh):
    in_specs = (
        P("fsdp", "ctx", None),
        P("fsdp", "ctx", None),
        P("fsdp", "ctx", None),
        P("fsdp", None, "ctx"),
        P("fsdp", None),
        P(),
        P(),
    )
    out_specs = (P("fsdp", None), P(), P(), P())
    return jax.shard_map(local, mesh=mesh, in_specs=in_specs, out_specs=out_specs, check_vma=False)
```

```python
import functools
import math

import jax
import jax.numpy as jnp
from jax import lax
from jax.experimental import pallas as pl
from jax.experimental.pallas import tpu as pltpu
from jax.sharding import PartitionSpec as P

HIGHEST = lax.Precision.HIGHEST
MESH = pl.DeviceIdType.MESH
F32 = jnp.float32
BF16 = jnp.bfloat16
T = 128
N = 64
GROUP = 4
ROW_CHIPS = 4


def dot(left, right):
    return jnp.dot(left, right, preferred_element_type=F32)


def dot_last(left, right):
    return lax.dot_general(left, right, (((1,), (1,)), ((), ())), preferred_element_type=F32)


def body(
    shards, blocks, scale,
    hid_h, val_h, tgt_h, dt_h, w_h, a_ref, skip_ref, ow, osc,
    hid, val, tgt, dt, in_sem, wbuf, hq, ws, dcb, bs, rate_s, step_s, decay_s, fin_s, we_s, alog_s, skip_s, loss_s,
    fin_sib, early_s, late_s, carry_out, carry_in,
    l_out, l_sib, s_raw, s_pass, s_in, e_out, e_sib, x_raw, x_pass, x_in,
    l_pair, l_in, s_out, e_pair, e_in, x_out,
    sg, acc_c, acc_b, pg_out, pg_in, r_out, r_in, c_out, c_in, y_out, y_in, z_out, z_in, d_out, d_in, t_out, t_in,
    w_send, w_recv, v_send, v_recv, u_send, h_send, h_fwd, h_recv, n_send, n_recv, k_send, k_recv,
    l_send, l_recv, s_send, s_recv, e_send, e_recv, x_send, x_recv,
    lp_send, lp_recv, sp_send, sp_recv, ep_send, ep_recv, xp_send, xp_recv,
    p_send, p_recv, r_send, r_recv, c_send, c_recv, y_send, y_recv, z_send, z_recv,
    d_send, d_recv, t_send, t_recv,
):
    heads = dt.shape[0]
    wide = w_h.shape[0]
    part = wide // (2 * ROW_CHIPS)
    chips = ROW_CHIPS
    octet = 2 * chips
    rows = blocks // octet
    f = lax.axis_index("fsdp")
    k = lax.axis_index("ctx")
    c = lax.rem(k, 2)
    o = lax.rem(k, octet)
    yh = lax.div(k, octet)
    x = lax.div(o, 2)
    first = yh * octet
    sib = k + 1 - 2 * c
    pairs = blocks // 2
    q = lax.div(k, 2)

    def mine(p):
        return 2 * p + c

    def theirs(p):
        return 2 * p + 1 - c

    def by_core(own_first, own_second):
        return jnp.where(c == 0, own_first, own_second)


    def ring(start, hop, count):
        return lax.rem(start + hop, count)

    def remote(src, dst, ss, rs, to_f, to_k):
        return pltpu.make_async_remote_copy(
            src_ref=src, dst_ref=dst, send_sem=ss, recv_sem=rs,
            device_id=(to_f, to_k), device_id_type=MESH,
        )

    def arrived(dst, rs):
        remote(dst, dst, rs, rs, f, sib).wait_recv()

    def left(src, ss):
        remote(src, src, ss, ss, f, sib).wait_send()

    def loop(count, fn, start=0):
        def step(i, carry):
            fn(i)
            return carry

        lax.fori_loop(start, count, step, 0)

    def lanes(i):
        return pl.ds(pl.multiple_of(i * T, T), T)

    barrier = pltpu.get_barrier_semaphore()

    def greet_f(j):
        pl.semaphore_signal(barrier, inc=1, device_id=(ring(f, j, shards), k), device_id_type=MESH)

    def greet_k(j):
        pl.semaphore_signal(barrier, inc=1, device_id=(f, mine(ring(q, j, pairs))), device_id_type=MESH)

    def greet_run(j):
        pl.semaphore_signal(barrier, inc=1, device_id=(f, first + theirs(j)), device_id_type=MESH)

    loop(shards, greet_f, 1)
    loop(pairs, greet_k, 1)
    loop(chips, greet_run)
    loads = [
        pltpu.make_async_copy(src, dst, in_sem.at[i])
        for i, (src, dst) in enumerate(((dt_h, dt), (val_h, val), (tgt_h, tgt), (hid_h, hid)), 1)
    ]
    for load in loads:
        load.start()
    pl.semaphore_wait(barrier, shards + pairs + chips - 2)

    own_part = pl.ds(pl.multiple_of(o * part, part), part)

    def w_go(j):
        remote(w_h.at[own_part], wbuf.at[f, own_part], w_send, w_recv.at[f], ring(f, j, shards), k).start()

    loop(shards, w_go, 1)
    own_copy = pltpu.make_async_copy(w_h.at[own_part], wbuf.at[f, own_part], in_sem.at[0])
    own_copy.start()

    loads[0].wait()

    def spread(h):
        rate_s[pl.ds(h, 1), :] = jnp.full((1, T), a_ref[h], F32)

    loop(heads, spread)
    step = jnp.maximum(dt[...], 0.0) + jnp.log1p(jnp.exp(-jnp.abs(dt[...])))
    row_id = lax.broadcasted_iota(jnp.int32, (T, T), 0)
    col_id = lax.broadcasted_iota(jnp.int32, (T, T), 1)
    upper = jnp.where(row_id <= col_id, 1.0, 0.0).astype(F32)
    decay = jnp.dot(-step * jnp.exp(rate_s[...]), upper, precision=HIGHEST, preferred_element_type=F32)
    fin = jnp.broadcast_to(decay[:, T - 1 :], (heads, T))
    step_s[...] = step
    decay_s[...] = decay
    fin_s[...] = fin
    we_s[...] = jnp.exp(fin - decay) * step

    remote(fin_s, fin_sib, n_send, n_recv, f, sib).start()

    def w_pass(j):
        g = ring(f, shards - j, shards)
        slot = wbuf.at[g, own_part]

        @pl.when(j > 0)
        def _():
            arrived(slot, w_recv.at[g])

        for hop in range(1, chips):
            there = first + ring(x, hop, chips) * 2 + c
            remote(slot, slot, v_send, v_recv.at[o], f, there).start()

    own_copy.wait()
    loop(shards, w_pass)
    own_slab = wbuf.at[:, own_part]
    remote(own_slab, own_slab, u_send, v_recv.at[o], f, sib).start()

    arrived(fin_sib, n_recv)
    early_s[...] = jnp.exp(by_core(fin_s[...], fin_sib[...]))
    late_s[...] = jnp.exp(by_core(fin_sib[...], fin_s[...]))

    def carry_go(p):
        h = mine(p)
        both = early_s[pl.ds(h, 1), :] * late_s[pl.ds(h, 1), :]
        carry_out[p] = jnp.broadcast_to(both, (8, T))

        @pl.when(p != q)
        def _():
            remote(carry_out.at[p], carry_in.at[q], k_send, k_recv.at[q], f, h).start()

        @pl.when(p == q)
        def _():
            carry_in[p] = carry_out[p]

    loop(pairs, carry_go)

    own_rows = pl.ds(pl.multiple_of(o * T, T), T)

    near_end, mid_end = shards * 3 // 8, shards * 3 // 4

    def h_go(i):
        part = jnp.where(i < mid_end, 0, octet)
        for hop in range(1, chips):
            there = ring(x, hop, chips)
            remote(
                hid.at[:, pl.ds(pl.multiple_of(i * wide + there * T, T), T)], hq.at[own_rows, lanes(i)],
                h_send, h_recv.at[part + o], f, first + there * 2 + c,
            ).start()

    def h_keep(i):
        hq[own_rows, lanes(i)] = hid[:, pl.ds(pl.multiple_of(i * wide + x * T, T), T)]

    def h_slab(src, late):
        start, size = (mid_end, shards - mid_end) if late else (0, mid_end)
        return hq.at[pl.ds(pl.multiple_of(src * T, T), T), pl.ds(start * T, size * T)]

    def h_next(src, late):
        there = h_recv.at[src + (octet if late else 0)]
        remote(h_slab(src, late), h_slab(src, late), h_fwd, there, f, sib).start()

    def h_pass(late):
        for hop in range(1, chips):
            src = ring(x, hop, chips) * 2 + c
            arrived(h_slab(src, late), h_recv.at[src + (octet if late else 0)])
            h_next(src, late)

    loads[3].wait()
    loop(near_end, h_go)
    loop(shards, h_keep)
    h_next(o, False)
    h_next(o, True)

    loads[1].wait()
    loads[2].wait()
    lower = row_id >= col_id

    def head_start(i):
        for u in range(GROUP):
            head_start_one(i * GROUP + u)

    def head_start_one(h):
        drow = decay_s[pl.ds(h, 1), :]
        col = jnp.transpose(jnp.broadcast_to(drow, (T, T)))
        dcb[h] = col
        within = jnp.where(lower, jnp.exp(jnp.minimum(col - drow, 0.0)), 0.0)
        ws[h] = within * step_s[pl.ds(h, 1), :]
        bs[h] = skip_ref[h] * val[:, lanes(h)].astype(F32) - tgt[:, lanes(h)].astype(F32)

    loop(heads // GROUP, head_start)

    def slab(src):
        return wbuf.at[:, pl.ds(pl.multiple_of(src * part, part), part)]

    for hop in range(1, chips):
        src = ring(x, hop, chips) * 2 + c
        arrived(slab(src), v_recv.at[src])
        remote(slab(src), slab(src), u_send, v_recv.at[src], f, sib).start()

    def w_rest(j):
        src = j * 2 + 1 - c
        arrived(slab(src), v_recv.at[src])

    loop(chips, w_rest)
    proj = dot(hid[...], wbuf[...].reshape(shards * wide, 2 * N))
    proj = proj.astype(BF16).astype(F32)
    proj_t = jnp.transpose(proj)
    map_bt = proj_t[:N]
    map_b_t = proj_t[:N].astype(BF16)
    map_c_t = proj_t[N:].astype(BF16)
    map_c = proj[:, N:].astype(BF16)
    scores = dot(map_c, map_b_t)

    def target(group, u):
        return ring(q, group * GROUP + u + 1, pairs)

    def origin(group, u):
        return ring(q, pairs - 1 - group * GROUP - u, pairs)

    def hand_over(p, out, come, send_sem, recv_sem):
        @pl.when(p != q)
        def _():
            remote(out.at[p], come.at[q], send_sem, recv_sem.at[q], f, mine(p)).start()

        @pl.when(p == q)
        def _():
            come[p] = out[p]

    def head_local_theirs(i):
        for u in range(GROUP):
            head_local_one(theirs(target(i, u)))
        for u in range(GROUP):
            h = theirs(target(i, u))
            remote(l_out.at[h], l_sib.at[h], lp_send, lp_recv.at[h], f, sib).start()

    def head_local_mine(i):
        for u in range(GROUP):
            head_local_one(mine(target(i, u)))
        for u in range(GROUP):
            p = target(i, u)
            h = mine(p)
            arrived(l_sib.at[h], lp_recv.at[h])
            own, other = l_out[h].astype(F32), l_sib[h].astype(F32)
            joined = late_s[pl.ds(h, 1), :] * by_core(own, other) + by_core(other, own)
            l_pair[p] = joined.astype(BF16)
            hand_over(p, l_pair, l_in, l_send, l_recv)

    def head_local_one(h):
        v = val[:, lanes(h)]
        mixing = (ws[h] * scores).astype(BF16)
        coef = (map_bt * we_s[pl.ds(h, 1), :]).astype(BF16)
        both = dot(jnp.concatenate([mixing, coef], axis=0), v)
        bs[h] = bs[h] + both[:T]
        l_out[h] = both[T:].astype(BF16)

    loop(pairs // GROUP, head_local_theirs)
    loop(pairs // GROUP, head_local_mine)

    def carry_wait(j):
        g = ring(q, j, pairs)
        arrived(carry_in.at[g], k_recv.at[g])

    loop(pairs, carry_wait, 1)

    def chain(came, out, back, in_sem, send_sem, back_sem, backward):
        def link(i, state):
            b = pairs - 1 - i if backward else i
            out[b] = state.astype(BF16)

            @pl.when(b != q)
            def _():
                arrived(came.at[b], in_sem.at[b])

            return carry_in[b, 0:1, :] * state + came[b].astype(F32)

        lax.fori_loop(0, pairs, link, jnp.zeros((N, T), F32))

        def give(j):
            b = ring(q, j, pairs)
            remote(out.at[b], back.at[k], send_sem, back_sem.at[k], f, mine(b)).start()

        loop(pairs, give, 1)
        back[k] = out[q]

    chain(l_in, s_out, s_raw, l_recv, s_send, s_recv, False)
    loop(mid_end, h_go, near_end)

    sg[...] = jnp.zeros_like(sg)
    acc_c[...] = jnp.zeros_like(acc_c)
    acc_b[...] = jnp.zeros_like(acc_b)

    def await_head(h, back, sem):
        @pl.when(h != k)
        def _():
            arrived(back.at[h], sem.at[h])

    def error_group(hs):
        parts = [head_error_one(h) for h in hs]
        sg[...] += sum(p[0] for p in parts)
        acc_c[...] += sum(p[1] for p in parts)

    def entries(i):
        for u in range(GROUP):
            p = origin(i, u)
            h = mine(p)
            arrived(e_sib.at[h], ep_recv.at[h])
            own, other = e_out[h].astype(F32), e_sib[h].astype(F32)
            joined = by_core(own, other) + early_s[pl.ds(h, 1), :] * by_core(other, own)
            e_pair[p] = joined.astype(BF16)
            hand_over(p, e_pair, e_in, e_send, e_recv)

    def head_error(i):
        hs = [mine(origin(i, u)) for u in range(GROUP)]
        for h in hs:
            await_head(h, s_raw, s_recv)
        for h in hs:
            state = s_raw[h].astype(F32)
            first_local = by_core(l_out[h], l_sib[h]).astype(F32)
            after = early_s[pl.ds(h, 1), :] * state + first_local
            s_in[h] = by_core(state, after).astype(BF16)
            s_pass[h] = by_core(after, state).astype(BF16)
            remote(s_pass.at[h], s_in.at[h], sp_send, sp_recv.at[h], f, sib).start()
        error_group(hs)

        @pl.when(i > 0)
        def _():
            entries(i - 1)

        hs = [theirs(origin(i, u)) for u in range(GROUP)]
        for h in hs:
            arrived(s_in.at[h], sp_recv.at[h])
        error_group(hs)
        for h in hs:
            remote(e_out.at[h], e_sib.at[h], ep_send, ep_recv.at[h], f, sib).start()

    def head_error_one(h):
        v = val[:, lanes(h)]
        state = s_in[h]
        col = dcb[h]
        growth = jnp.exp(col)
        grown_state = growth * dot(map_c, state)
        err = bs[h] + grown_state
        grad = err * scale
        loss_s[pl.ds(h, 1), :] = jnp.sum(err * err, axis=0, keepdims=True)
        skip_s[pl.ds(h, 1), :] = jnp.sum(grad * v.astype(F32), axis=0, keepdims=True)
        mix_grad = ws[h] * dot_last(grad.astype(BF16), v)
        turn = mix_grad * scores * (col - decay_s[pl.ds(h, 1), :]) + grad * grown_state * col
        alog_s[pl.ds(h, 1), :] = jnp.sum(turn, axis=0, keepdims=True)
        grown = (growth * grad).astype(BF16)
        e_out[h] = dot(map_c_t, grown).astype(BF16)
        return mix_grad, dot_last(state, grown)

    loop(pairs // GROUP, head_error)
    entries(pairs // GROUP - 1)

    h_pass(False)

    chain(e_in, x_out, x_raw, e_recv, x_send, x_recv, True)
    loop(shards, h_go, mid_end)

    def head_exit(i):
        hs = [mine(origin(i, u)) for u in range(GROUP)]
        for h in hs:
            await_head(h, x_raw, x_recv)
        for h in hs:
            exit_late = x_raw[h].astype(F32)
            entry_late = by_core(e_sib[h], e_out[h]).astype(F32)
            exit_early = entry_late + late_s[pl.ds(h, 1), :] * exit_late
            x_in[h] = by_core(exit_early, exit_late).astype(BF16)
            x_pass[h] = by_core(exit_late, exit_early).astype(BF16)
            remote(x_pass.at[h], x_in.at[h], xp_send, xp_recv.at[h], f, sib).start()
        acc_b[...] += sum(head_exit_one(h) for h in hs)
        hs = [theirs(origin(i, u)) for u in range(GROUP)]
        for h in hs:
            arrived(x_in.at[h], xp_recv.at[h])
        acc_b[...] += sum(head_exit_one(h) for h in hs)

    def head_exit_one(h):
        leaving = x_in[h]
        last = fin_s[pl.ds(h, 1), :]
        weighed = dot_last(leaving, val[:, lanes(h)]) * we_s[pl.ds(h, 1), :]
        end = jnp.sum(weighed * map_bt, axis=0, keepdims=True)
        kept = jnp.sum(leaving.astype(F32) * s_in[h].astype(F32), axis=0, keepdims=True)
        alog_s[pl.ds(h, 1), :] += end * (last - decay_s[pl.ds(h, 1), :]) + last * jnp.exp(last) * kept
        return weighed

    loop(pairs // GROUP, head_exit)

    score_bf = sg[...].astype(BF16)
    pg_out[0] = (dot(map_c_t, score_bf) + acc_b[...]).astype(BF16)
    pg_out[1] = (dot_last(map_b_t, score_bf) + acc_c[...]).astype(BF16)
    own_cols = lanes(o)

    def pg_go(j):
        there = ring(o, j, octet)
        remote(
            pg_out.at[lax.rem(there, 2)], pg_in.at[:, own_cols], p_send, p_recv.at[o], f, first + there
        ).start()

    loop(octet, pg_go, 1)
    pg_in[:, own_cols] = pg_out[c]

    alog = jnp.sum(alog_s[...], axis=1, keepdims=True)
    skip = jnp.sum(skip_s[...], axis=1, keepdims=True)
    loss = jnp.sum(loss_s[...], axis=1, keepdims=True) * (0.5 * scale)
    lane = lax.broadcasted_iota(jnp.int32, (heads, T), 1)
    tile = jnp.where(lane == 0, alog, jnp.where(lane == 1, skip, jnp.where(lane == 2, loss, 0.0)))
    square = jnp.concatenate([tile, jnp.zeros((T - heads, T), F32)], axis=0)
    c_out[...] = jnp.transpose(square)[0:8]

    def c_go(j):
        remote(c_out, c_in.at[f], c_send, c_recv.at[f], ring(f, j, shards), k).start()

    loop(shards, c_go, 1)
    c_in[f] = c_out[...]

    h_pass(True)

    def h_wait(j):
        src = j * 2 + 1 - c
        arrived(h_slab(src, False), h_recv.at[src])
        arrived(h_slab(src, True), h_recv.at[octet + src])

    loop(chips, h_wait)

    def pg_wait(j):
        src = ring(o, j, octet)
        arrived(pg_in.at[:, lanes(src)], p_recv.at[src])

    loop(octet, pg_wait, 1)

    def r_go(j):
        two = ring(lax.div(f, 2), j, shards // 2)
        product = dot(pg_in[...], hq[:, pl.ds(pl.multiple_of(two * 2 * T, 2 * T), 2 * T)]).astype(BF16)
        for u in range(2):
            g = two * 2 + u
            r_out[g] = product[:, u * T : (u + 1) * T]

            @pl.when(g != f)
            def _():
                remote(r_out.at[g], r_in.at[f], r_send, r_recv.at[f], g, k).start()

            @pl.when(g == f)
            def _():
                r_in[g] = r_out[g]

    loop(shards // 2 + 1, r_go, 1)

    def r_wait(j):
        g = ring(f, j, shards)
        arrived(r_in.at[g], r_recv.at[g])
        arrived(c_in.at[g], c_recv.at[g])

    loop(shards, r_wait, 1)
    total = r_in[0].astype(F32)
    sums = c_in[0]
    for i in range(1, shards):
        total = total + r_in[i].astype(F32)
        sums = sums + c_in[i]
    y_out[...] = total.astype(BF16)
    d_out[...] = sums

    for hop in range(1, rows):
        there = ring(yh, hop, rows) * octet + o
        remote(y_out, y_in.at[yh], y_send.at[hop], y_recv.at[yh], f, there).start()
        remote(d_out, d_in.at[yh], d_send.at[hop], d_recv.at[yh], f, there).start()
    y_in[yh] = y_out[...]
    d_in[yh] = d_out[...]
    for hop in range(1, rows):
        src = ring(yh, hop, rows)
        arrived(y_in.at[src], y_recv.at[src])
        arrived(d_in.at[src], d_recv.at[src])
    total = y_in[0].astype(F32)
    sums = d_in[0]
    for i in range(1, rows):
        total = total + y_in[i].astype(F32)
        sums = sums + d_in[i]
    z_out[...] = total.astype(BF16)
    t_out[...] = sums

    def z_go(j):
        there = first + ring(o, j, octet)
        remote(z_out, z_in.at[o], z_send, z_recv.at[o], f, there).start()
        remote(t_out, t_in.at[o], t_send, t_recv.at[o], f, there).start()

    loop(octet, z_go, 1)
    z_in[o] = z_out[...]
    t_in[o] = t_out[...]

    def z_wait(j):
        src = ring(o, j, octet)
        arrived(z_in.at[src], z_recv.at[src])
        arrived(t_in.at[src], t_recv.at[src])

    loop(octet, z_wait, 1)
    for i in range(chips):
        ow[i * T : (i + 1) * T, :] = jnp.transpose(
            jnp.concatenate([z_in[2 * i], z_in[2 * i + 1]], axis=0).astype(F32)
        )
    sums = t_in[0]
    for i in range(1, octet):
        sums = sums + t_in[i]
    osc[...] = sums

    others = pl.ds(0, pairs - 1)
    every = pl.ds(0, pairs)
    peers = pl.ds(0, shards - 1)
    left(wbuf.at[peers, pl.ds(0, part)], w_send)
    left(wbuf.at[:, pl.ds(0, (chips - 1) * part)], v_send)
    left(wbuf.at[:, pl.ds(0, chips * part)], u_send)
    left(hq.at[pl.ds(0, (chips - 1) * T)], h_send)
    left(hq.at[pl.ds(0, chips * T)], h_fwd)
    left(carry_out.at[others], k_send)
    left(fin_s, n_send)
    left(l_pair.at[others], l_send)
    left(s_out.at[others], s_send)
    left(e_pair.at[others], e_send)
    left(x_out.at[others], x_send)
    left(l_out.at[every], lp_send)
    left(s_pass.at[every], sp_send)
    left(e_out.at[every], ep_send)
    left(x_pass.at[every], xp_send)
    left(pg_in.at[:, pl.ds(0, (octet - 1) * T)], p_send)
    left(r_out.at[peers], r_send)
    left(c_in.at[peers], c_send)
    for hop in range(1, rows):
        left(y_out, y_send.at[hop])
        left(d_out, d_send.at[hop])
    left(z_in.at[pl.ds(0, octet - 1)], z_send)
    left(t_in.at[pl.ds(0, octet - 1)], t_send)


def local(hidden, values, targets, dt_raw, proj_weight, a_log, skip):
    shards = lax.axis_size("fsdp")
    blocks = lax.axis_size("ctx")
    heads = a_log.shape[0]
    wide, both = proj_weight.shape
    octet = 2 * ROW_CHIPS
    rows = blocks // octet
    scale = 1.0 / (values.shape[2] * math.sqrt(shards * hidden.shape[1] * blocks))
    vmem = pltpu.VMEM
    per_head = lambda kind: vmem((heads, N, T), kind)
    small = vmem((heads, T), F32)
    one = pltpu.SemaphoreType.DMA
    many = lambda n: pltpu.SemaphoreType.DMA((n,))
    scratch = [
        vmem(hidden.shape[1:], BF16), vmem(values.shape[1:], BF16), vmem(targets.shape[1:], BF16),
        small, many(5),
        vmem((shards, wide, both), BF16),
        vmem((octet * T, shards * T), BF16),
        vmem((heads, T, T), F32), vmem((heads, T, T), F32), vmem((heads, T, T), F32),
        *[small] * 8,
        small, small, small, vmem((blocks // 2, 8, T), F32), vmem((blocks // 2, 8, T), F32),
        *[per_head(BF16)] * 10,
        *[vmem((blocks // 2, N, T), BF16)] * 6,
        vmem((T, T), F32), vmem((N, T), F32), vmem((N, T), F32),
        vmem((2, N, T), BF16), vmem((N, octet * T), BF16),
        vmem((shards, N, T), BF16), vmem((shards, N, T), BF16),
        vmem((8, T), F32), vmem((shards, 8, T), F32),
        vmem((N, T), BF16), vmem((rows, N, T), BF16),
        vmem((N, T), BF16), vmem((octet, N, T), BF16),
        vmem((8, T), F32), vmem((rows, 8, T), F32), vmem((8, T), F32), vmem((octet, 8, T), F32),
        one, many(shards), one, many(octet), one, one, one, many(2 * octet), one, one, one, many(blocks),
        *[one, many(blocks)] * 8,
        one, many(octet), one, many(shards), one, many(shards), many(rows), many(rows), one, many(octet),
        many(rows), many(rows), one, many(octet),
    ]
    spec = pl.BlockSpec(memory_space=vmem)
    grad_w, sums = pl.pallas_call(
        functools.partial(body, shards, blocks, scale),
        out_shape=(
            jax.ShapeDtypeStruct((wide, both), F32),
            jax.ShapeDtypeStruct((8, T), F32),
        ),
        in_specs=[pl.BlockSpec(memory_space=pltpu.HBM)] * 5 + [pl.BlockSpec(memory_space=pltpu.SMEM)] * 2,
        out_specs=(spec, spec),
        scratch_shapes=scratch,
        compiler_params=pltpu.CompilerParams(
            collective_id=0, has_side_effects=True, vmem_limit_bytes=56 * 2**20
        ),
    )(hidden[0], values[0], targets[0], dt_raw[0], proj_weight, a_log, skip)
    return (grad_w, sums[0, :heads], sums[1, :heads], jnp.sum(sums[2, :heads]))


def solution(mesh):
    in_specs = (
        P("fsdp", "ctx", None),
        P("fsdp", "ctx", None),
        P("fsdp", "ctx", None),
        P("fsdp", None, "ctx"),
        P("fsdp", None),
        P(),
        P(),
    )
    out_specs = (P("fsdp", None), P(), P(), P())
    return jax.shard_map(local, mesh=mesh, in_specs=in_specs, out_specs=out_specs, check_vma=False)
```
